256 devices in a mesh: trow: 32 (over z, x), mode: 8 (over y, core).
Axes of the slice: x: 4, y: 4, z: 8, core: 2. Of those that a mesh axis runs over, the one named last changes fastest.
Arguments:
- g_hist: bfloat16 [2, 64, 64, 128, 128], P(None, 'trow', None, 'mode'), may hold values from -4 to 4
- new_cols: bfloat16 [2, 64, 8, 128, 128], P(None, 'trow', None, 'mode'), may hold values from -4 to 4
- row_time: int32 [64], replicated, may hold values from 0 to 63, as said below
- drive_step: int32 [64], replicated, may hold values from 0 to 15
- drive_levels: float32 [16, 128], replicated, may hold values from 0.5 to 1.5
Outputs:
- collision: float32 [2, 64, 8, 128, 128], P(None, 'trow', None, 'mode')
The draws below stay inside these ranges and needn't reach their ends.
Inputs may be any that keep to these rules, and one draw needn't show every extreme that they name: `row_time`: the 2 row slots of one index of trow hold 2 consecutive times in rising order, the first a multiple of 2; every time is held by exactly one slot.
All inputs are finite; a program needn't handle non-finite values.
Results may differ from the reference program's by a relative error of at most 0.0029.
Values may be sent and summed in bfloat16 or wider, within the bound.
A program may use at most 128 MiB of HBM per device.

```python
import math
import jax
import jax.numpy as jnp
from jax import lax

M = 128
ROWS = 2
NC = 8
LEVELS = 16
NT = 64


def draw_row_time(key, part):
    key = jax.random.fold_in(key, 7)
    block_order = jax.random.permutation(key, NT // ROWS).astype(jnp.int32)
    within = jnp.arange(ROWS, dtype=jnp.int32)
    return (block_order[:, None] * ROWS + within[None, :]).reshape(NT).astype(jnp.int32)


def with_ends(values, key, least, largest):
    spot = [jax.random.randint(jax.random.fold_in(key, axis), (), 0, length) for axis, length in enumerate(values.shape)]
    main_axis = values.shape.index(max(values.shape))
    neighbour = spot[:main_axis] + [(spot[main_axis] + 1) % values.shape[main_axis]] + spot[main_axis + 1:]
    return values.at[tuple(spot)].set(least).at[tuple(neighbour)].set(largest)


def block_levels(own_key, shape, split, smallest, high):
    gain = 1.0
    for position, parts in split:
        heights = jax.random.uniform(jax.random.fold_in(jax.random.fold_in(own_key, 6), position), (parts,), jnp.float32, smallest / len(split), high / len(split))
        gain = gain * jnp.repeat(jnp.exp(heights), shape[position] // parts).reshape((-1,) + (1,) * (len(shape) - 1 - position))
    return gain


def normal_values(own_key, dims, deviation, limit, shards=(), held_as=jnp.bfloat16):
    entries = jax.random.normal(own_key, dims, jnp.float32) * deviation
    if len(shards) > 0:
        entries = block_levels(own_key, dims, shards, -0.22, 0.18) * entries
    return jnp.clip(entries, min=-limit, max=limit).astype(held_as)


def setup_inputs(seed: int = 0) -> dict:
    key_list = jax.random.split(jax.random.key(seed), 6)
    g_hist = normal_values(key_list[0], (2, NT, NT, M, M), 0.5, 4.0, ((1, 32), (3, 8)))
    new_cols = normal_values(key_list[1], (2, NT, NC, M, M), 0.5, 4.0, ((1, 32), (3, 8)))
    row_time = draw_row_time(jax.random.fold_in(key_list[5], 71), 0)
    drive_step = with_ends(jax.random.randint(key_list[3], (NT,), 0, LEVELS), jax.random.fold_in(key_list[3], 1), 0, LEVELS - 1).astype(jnp.int32)
    drive_levels = jnp.clip(jnp.exp(jax.random.uniform(key_list[4], (LEVELS, M), jnp.float32, math.log(0.5), math.log(1.5))), 0.5, 1.5)
    return dict(g_hist=g_hist, new_cols=new_cols, row_time=row_time, drive_step=drive_step, drive_levels=drive_levels)


TIME_SPAN = 8.0


def reference(g_hist, new_cols, row_time, drive_step, drive_levels):
    kerr_time = drive_levels[drive_step]
    kerr_slot = kerr_time[row_time]
    column_re = new_cols[0].astype(jnp.float32)
    column_im = new_cols[1].astype(jnp.float32)
    live_all = row_time

    def one_row(row_slot):
        time_now = row_time[row_slot]
        own_row = lax.dynamic_index_in_dim(g_hist, row_slot, axis=1, keepdims=False)
        own_row = jnp.take(own_row, row_time, axis=1).astype(jnp.float32)
        mirror = lax.dynamic_index_in_dim(g_hist, time_now, axis=2, keepdims=False).astype(jnp.float32)
        mirror = jnp.swapaxes(mirror, 2, 3)
        green_re = own_row[0]
        green_im = own_row[1]
        mirror_re = mirror[0]
        mirror_im = mirror[1]
        square_re = green_re * green_re - green_im * green_im
        square_im = 2.0 * green_re * green_im
        bubble_re = square_re * mirror_re - square_im * mirror_im
        bubble_im = square_re * mirror_im + square_im * mirror_re
        coupling = lax.dynamic_index_in_dim(kerr_slot, row_slot, axis=0, keepdims=False)[None, None, :] * kerr_slot[:, :, None]
        live = (live_all <= time_now)[:, None, None]
        sigma_re = jnp.where(live, bubble_re * coupling, 0.0).astype(jnp.bfloat16)
        sigma_im = jnp.where(live, bubble_im * coupling, 0.0).astype(jnp.bfloat16)
        sigma_re = lax.optimization_barrier(sigma_re).astype(jnp.float32)
        sigma_im = lax.optimization_barrier(sigma_im).astype(jnp.float32)
        part_re = jnp.einsum("kyx,knyb->nxb", sigma_re, column_re) - jnp.einsum("kyx,knyb->nxb", sigma_im, column_im)
        part_im = jnp.einsum("kyx,knyb->nxb", sigma_re, column_im) + jnp.einsum("kyx,knyb->nxb", sigma_im, column_re)
        step_size = TIME_SPAN / NT
        return jnp.stack([step_size * part_re, step_size * part_im])

    result = lax.map(one_row, jnp.arange(NT, dtype=jnp.int32))
    return jnp.swapaxes(result, 0, 1)
```

```python
import jax
import jax.numpy as jnp
from jax import lax
from jax.experimental import pallas as pl
from jax.experimental.pallas import tpu as pltpu
from jax.sharding import PartitionSpec as P

NZ, NX, NY, NCORE = 8, 4, 4, 2
NR, NMODE = NZ * NX, NY * NCORE
BF, F32 = jnp.bfloat16, jnp.float32
MESH = pl.DeviceIdType.MESH

DZ = (4, 3, 5, 2, 6, 1, 7, 0)
A1, A2 = (0, 384), (384, 384)
A = (0, 768)
B1, B2 = (768, 128), (896, 128)
B = (768, 256)
SCALE = 8.0 / 64


def kernel(
    rt, ds, dl, g, c, out,
    sb, rb, tb, mb, sq, lhs, rhs, part, cb, red, yb, kb,
    s1_send, s1_recv, s2_send, s2_recv,
    za_s, za_r, xa_s, xa_r, xb_s, xb_r, zb_s, zb_r,
    cx_s, cx_r, yx_s, yx_r,
):
    r = lax.axis_index("trow")
    m = lax.axis_index("mode")
    z, x = r // NX, r % NX
    y, core = m // NCORE, m % NCORE

    def at_z(d):
        return (z + d + NZ) % NZ

    def at_x(d):
        return (x + d + NX) % NX

    def trow_dev(zz, xx):
        return {"trow": zz * NX + xx, "mode": m}

    bar = pltpu.get_barrier_semaphore()

    def greet_trow(j, _):
        pl.semaphore_signal(bar, inc=1, device_id={"trow": (r + 1 + j) % NR, "mode": m}, device_id_type=MESH)
        return 0

    def greet_mode(j, _):
        pl.semaphore_signal(bar, inc=1, device_id={"trow": r, "mode": (m + 1 + j) % NMODE}, device_id_type=MESH)
        return 0

    lax.fori_loop(0, NR - 1, greet_trow, 0)
    lax.fori_loop(0, NMODE - 1, greet_mode, 0)

    for p in range(2):
        for k in range(2):
            for n in range(8):
                rhs[z, p, x, pl.ds(16 * k, 16), pl.ds(128 * n, 128)] = c[p, k, n]

    def fill(q, _):
        for i in range(2):
            t = rt[2 * q + i]
            for p in range(2):
                for o in range(2):
                    sb[q, p, i, o] = g[p, o, t]
        return 0

    lax.fori_loop(0, NR, fill, 0)
    rb[r] = sb[r]

    pl.semaphore_wait(bar, NR - 1 + NMODE - 1)

    sent = []

    def push(zz, xx, lanes, s, rsem, dev):
        ref = rhs.at[zz, :, xx, :, pl.ds(*lanes)] if xx is not None else rhs.at[zz, :, :, :, pl.ds(*lanes)]
        d = pltpu.make_async_remote_copy(ref, ref, s, rsem, device_id=dev, device_id_type=MESH)
        d.start()
        sent.append(d)

    def landed(zz, xx, lanes, rsem):
        ref = rhs.at[zz, :, xx, :, pl.ds(*lanes)] if xx is not None else rhs.at[zz, :, :, :, pl.ds(*lanes)]
        pltpu.make_async_copy(ref, ref, rsem).wait()

    up, down = trow_dev(at_z(1), x), trow_dev(at_z(-1), x)
    right, left = trow_dev(z, at_x(1)), trow_dev(z, at_x(-1))

    def a_z_send(t):
        lo, hi = (A, A) if t < 4 else (A1, A2)
        push(at_z(-(t - 1)), x, lo, za_s.at[0, t - 1], za_r.at[0, t - 1], up)
        push(at_z(t - 1), x, hi, za_s.at[1, t - 1], za_r.at[1, t - 1], down)

    def a_z_wait(t):
        lo, hi = (A, A) if t < 4 else (A1, A2)
        landed(at_z(-t), x, lo, za_r.at[0, t - 1])
        landed(at_z(t), x, hi, za_r.at[1, t - 1])

    def a_x_send(d):
        zz, e = at_z(d), d % NZ
        push(zz, x, A, xa_s.at[e, 0], xa_r.at[e, 0], right)
        push(zz, x, A, xa_s.at[e, 1], xa_r.at[e, 1], left)

    def a_x_forward(d):
        zz, e = at_z(d), d % NZ
        landed(zz, at_x(-1), A, xa_r.at[e, 0])
        push(zz, at_x(-1), A1, xa_s.at[e, 2], xa_r.at[e, 2], right)
        landed(zz, at_x(1), A, xa_r.at[e, 1])
        push(zz, at_x(1), A2, xa_s.at[e, 3], xa_r.at[e, 3], left)

    def a_x_last(d):
        zz, e = at_z(d), d % NZ
        landed(zz, at_x(2), A1, xa_r.at[e, 2])
        landed(zz, at_x(2), A2, xa_r.at[e, 3])

    def b_x_send():
        push(z, x, B, xb_s.at[0], xb_r.at[0], right)
        push(z, x, B, xb_s.at[1], xb_r.at[1], left)

    def b_x_forward():
        landed(z, at_x(-1), B, xb_r.at[0])
        push(z, at_x(-1), B1, xb_s.at[2], xb_r.at[2], right)
        landed(z, at_x(1), B, xb_r.at[1])
        push(z, at_x(1), B2, xb_s.at[3], xb_r.at[3], left)

    def b_x_last():
        landed(z, at_x(2), B1, xb_r.at[2])
        landed(z, at_x(2), B2, xb_r.at[3])

    def b_z_send(t):
        lo, hi = (B, B) if t < 4 else (B1, B2)
        push(at_z(-(t - 1)), None, lo, zb_s.at[0, t - 1], zb_r.at[0, t - 1], up)
        push(at_z(t - 1), None, hi, zb_s.at[1, t - 1], zb_r.at[1, t - 1], down)

    def b_z_wait(t):
        lo, hi = (B, B) if t < 4 else (B1, B2)
        landed(at_z(-t), None, lo, zb_r.at[0, t - 1])
        landed(at_z(t), None, hi, zb_r.at[1, t - 1])

    def mirror_send(d):
        for e in range(NX):
            if d == 0 and e == 0:
                continue
            q = at_z(d) * NX + at_x(e)
            pltpu.make_async_remote_copy(
                sb.at[q], rb.at[r], s1_send.at[0], s1_recv.at[r],
                device_id={"trow": q, "mode": m}, device_id_type=MESH,
            ).start()

    lane_group = lax.broadcasted_iota(jnp.int32, (16, 128), 1) // 16

    def mirror_regroup(d):
        kg = at_z(-d)
        for e in range(NX):
            if d == 0 and e == 0:
                continue
            q = kg * NX + at_x(-e)
            pltpu.make_async_copy(rb.at[q], rb.at[q], s1_recv.at[q]).wait()

        def one(ps, _):
            p, s = ps // 2, ps % 2
            tiles = [rb[kg * NX + k // 2, p, s, k % 2].astype(F32) for k in range(8)]
            for bit in (1, 2, 4):
                has = (lane_group // bit) % 2 == 1
                new = list(tiles)
                for k in range(8):
                    if k & bit:
                        continue
                    a, b = tiles[k], tiles[k + bit]
                    new[k] = jnp.where(has, pltpu.roll(b, 16 * bit, 1), a)
                    new[k + bit] = jnp.where(has, b, pltpu.roll(a, 128 - 16 * bit, 1))
                tiles = new
            for j in range(8):
                tb[kg, j, p, s] = tiles[j].astype(BF)
            return 0

        lax.fori_loop(0, 4, one, 0)

        def send(j, _):
            to = (m + 1 + j) % NMODE
            pltpu.make_async_remote_copy(
                tb.at[kg, to], mb.at[kg, m], s2_send.at[0], s2_recv.at[kg, m],
                device_id={"trow": r, "mode": to}, device_id_type=MESH,
            ).start()
            return 0

        lax.fori_loop(0, NMODE - 1, send, 0)
        mb[kg, m] = tb[kg, m]

    def sigma(d):
        kg = at_z(-d)

        def arrive(j, _):
            q = (m + 1 + j) % NMODE
            pltpu.make_async_copy(mb.at[kg, q], mb.at[kg, q], s2_recv.at[kg, q]).wait()
            return 0

        lax.fori_loop(0, NMODE - 1, arrive, 0)
        base = pl.multiple_of(kg * 256, 256)
        for s in range(2):
            hr = mb[kg, :, 0, s].reshape(128, 128).astype(F32)
            hi = mb[kg, :, 1, s].reshape(128, 128).astype(F32)
            qr, qi = sq[kg, s, 0], sq[kg, s, 1]
            sr = qr * hr - qi * hi
            si = qr * hi + qi * hr
            lo, hi_lanes = pl.ds(base, 128), pl.ds(base + 128, 128)
            lhs[pl.ds(128 * s, 128), lo] = sr.astype(BF)
            lhs[pl.ds(128 * s, 128), hi_lanes] = (-si).astype(BF)
            lhs[pl.ds(256 + 128 * s, 128), lo] = si.astype(BF)
            lhs[pl.ds(256 + 128 * s, 128), hi_lanes] = sr.astype(BF)

    def squares():
        def strengths(k, _):
            t = rt[k]
            row = dl[pl.ds(ds[t], 1), :]
            for s in range(2):
                live = jnp.where(t <= rt[2 * r + s], 1.0, 0.0).astype(F32)
                kb[s, k % 8, pl.ds(k // 8, 1), :] = row * live
            return 0

        lax.fori_loop(0, 64, strengths, 0)
        group8 = lax.broadcasted_iota(jnp.int32, (8, 128), 1) // 16
        for s in range(2):
            rows = jnp.zeros((8, 128), F32)
            for k in range(8):
                turned = pltpu.roll(kb[s, k], (16 * k + 128 - 16 * m) % 128, 1)
                rows = jnp.where(group8 == k, turned, rows)
            kb[s, 8] = rows
        cols = []
        for s in range(2):
            row = dl[pl.ds(ds[rt[2 * r + s]], 1), :]
            cols.append(jnp.broadcast_to(row, (128, 128)).T)

        def one(kg, _):
            for s in range(2):
                coupling = cols[s] * kb[s, 8, pl.ds(kg, 1), :]
                gr = sb[pl.ds(kg * NX, NX), 0, :, s].reshape(128, 128).astype(F32).T
                gi = sb[pl.ds(kg * NX, NX), 1, :, s].reshape(128, 128).astype(F32).T
                sq[kg, s, 0] = (gr * gr - gi * gi) * coupling
                sq[kg, s, 1] = (2.0 * gr * gi) * coupling
            return 0

        lax.fori_loop(0, NZ, one, 0)

    a_z_send(1)
    b_x_send()
    a_x_send(0)
    mirror_send(DZ[0])
    mirror_send(DZ[1])
    squares()

    b_x_forward()
    a_z_wait(1)
    a_z_send(2)
    a_x_send(-1)
    a_x_send(1)
    mirror_send(DZ[2])
    a_x_forward(0)

    b_x_last()
    b_z_send(1)
    a_z_wait(2)
    a_z_send(3)
    a_x_send(-2)
    a_x_send(2)
    mirror_send(DZ[3])
    mirror_regroup(DZ[0])
    a_x_forward(-1)
    a_x_forward(1)

    b_z_wait(1)
    b_z_send(2)
    a_z_wait(3)
    a_z_send(4)
    a_x_send(-3)
    a_x_send(3)
    mirror_send(DZ[4])
    mirror_regroup(DZ[1])
    a_x_forward(-2)
    a_x_forward(2)

    b_z_wait(2)
    b_z_send(3)
    a_z_wait(4)
    a_x_send(4)
    mirror_send(DZ[5])
    mirror_regroup(DZ[2])
    sigma(DZ[0])
    a_x_forward(-3)
    a_x_forward(3)

    b_z_wait(3)
    b_z_send(4)
    mirror_send(DZ[6])
    mirror_send(DZ[7])
    mirror_regroup(DZ[3])
    sigma(DZ[1])
    a_x_forward(4)

    for i in range(4, 8):
        mirror_regroup(DZ[i])
        sigma(DZ[i - 2])
    sigma(DZ[6])
    sigma(DZ[7])
    b_z_wait(4)
    for d in range(NZ):
        a_x_last(d)

    def core_copy(j):
        return pltpu.make_async_remote_copy(
            part.at[:, pl.ds(2 * j, 2), :, 1 - core], cb.at[:, pl.ds(2 * j, 2)], cx_s.at[j], cx_r.at[j],
            device_id={"trow": r, "mode": y * NCORE + 1 - core}, device_id_type=MESH,
        )

    def y_copy(j, e):
        to = (y + e) % NY
        return pltpu.make_async_remote_copy(
            red.at[:, pl.ds(2 * j, 2), to], yb.at[e - 1, :, pl.ds(2 * j, 2)], yx_s.at[j, e - 1], yx_r.at[j, e - 1],
            device_id={"trow": r, "mode": to * NCORE + core}, device_id_type=MESH,
        )

    def multiply(j):
        cols = rhs[:, :, :, :, pl.ds(256 * j, 256)].reshape(2048, 256)
        for h in range(2):
            acc = jnp.dot(lhs[pl.ds(256 * h, 256), :], cols, preferred_element_type=F32)
            for s in range(2):
                for n in range(2):
                    part[2 * h + s, 2 * j + n] = acc[128 * s : 128 * (s + 1), 128 * n : 128 * (n + 1)].reshape(
                        NY, NCORE, 16, 128
                    )
        core_copy(j).start()

    def core_sum(j):
        core_copy(j).wait_recv()
        here = pl.ds(2 * j, 2)
        red[:, here] = part[:, here, :, core] + cb[:, here]
        for e in (2, 1, 3):
            y_copy(j, e).start()

    def y_sum(j):
        for e in (2, 1, 3):
            y_copy(j, e).wait_recv()
        here = pl.ds(2 * j, 2)
        total = red[:, here, y] + (yb[1, :, here] + (yb[0, :, here] + yb[2, :, here]))
        out[:, :, here] = (total * SCALE).reshape(2, 2, 2, 16, 128)

    for j in range(4):
        multiply(j)
        if j >= 1:
            core_sum(j - 1)
    core_sum(3)
    for j in range(4):
        y_sum(j)

    for d in sent:
        d.wait_send()
    all_but_one = sb.at[pl.ds(0, NR - 1)]
    pltpu.make_async_copy(all_but_one, all_but_one, s1_send.at[0]).wait()
    all_but_own = tb.at[:, pl.ds(0, NMODE - 1)]
    pltpu.make_async_copy(all_but_own, all_but_own, s2_send.at[0]).wait()
    for j in range(4):
        core_copy(j).wait_send()
        for e in (2, 1, 3):
            y_copy(j, e).wait_send()


def body(g_hist, new_cols, row_time, drive_step, drive_levels):
    smem = pl.BlockSpec(memory_space=pltpu.SMEM)
    vmem = pl.BlockSpec(memory_space=pltpu.VMEM)
    dma = pltpu.SemaphoreType.DMA
    return pl.pallas_call(
        kernel,
        out_shape=jax.ShapeDtypeStruct((2, 2, 8, 16, 128), F32),
        in_specs=[smem, smem, vmem, vmem, vmem],
        out_specs=vmem,
        scratch_shapes=[
            pltpu.VMEM((NR, 2, 2, 2, 16, 128), BF),
            pltpu.VMEM((NR, 2, 2, 2, 16, 128), BF),
            pltpu.VMEM((NZ, NMODE, 2, 2, 16, 128), BF),
            pltpu.VMEM((NZ, NMODE, 2, 2, 16, 128), BF),
            pltpu.VMEM((NZ, 2, 2, 128, 128), F32),
            pltpu.VMEM((512, 2048), BF),
            pltpu.VMEM((NZ, 2, NX, 32, 1024), BF),
            pltpu.VMEM((4, 8, NY, NCORE, 16, 128), F32),
            pltpu.VMEM((4, 8, NY, 16, 128), F32),
            pltpu.VMEM((4, 8, NY, 16, 128), F32),
            pltpu.VMEM((3, 4, 8, 16, 128), F32),
            pltpu.VMEM((2, 9, 8, 128), F32),
            dma((1,)), dma((NR,)), dma((1,)), dma((NZ, NMODE)),
            dma((2, 4)), dma((2, 4)), dma((NZ, 4)), dma((NZ, 4)),
            dma((4,)), dma((4,)), dma((2, 4)), dma((2, 4)),
            dma((4,)), dma((4,)), dma((4, 3)), dma((4, 3)),
        ],
        compiler_params=pltpu.CompilerParams(
            collective_id=0, has_side_effects=True, vmem_limit_bytes=40 * 1024 * 1024
        ),
        cost_estimate=pl.CostEstimate(flops=2147483648, bytes_accessed=1600000, transcendentals=0),
    )(row_time, drive_step, drive_levels, g_hist, new_cols)


def solution(mesh):
    placed = (
        P(None, "trow", None, "mode", None),
        P(None, "trow", None, "mode", None),
        P(),
        P(),
        P(),
    )
    return jax.shard_map(
        body,
        mesh=mesh,
        in_specs=placed,
        out_specs=P(None, "trow", None, "mode", None),
        check_vma=False,
    )
```

```python
import jax
import jax.numpy as jnp
from jax import lax
from jax.experimental import pallas as pl
from jax.experimental.pallas import tpu as pltpu
from jax.sharding import PartitionSpec as P

NZ, NX, NY, NCORE = 8, 4, 4, 2
NR, NMODE = NZ * NX, NY * NCORE
BF, F32 = jnp.bfloat16, jnp.float32
MESH = pl.DeviceIdType.MESH

CHUNK = ((3, 1), (3, 1))
PIECE = (4, 4)
YT = BF

SCALE = 8.0 / 64


def lanes(chunk, which):
    first = sum(a + b for a, b in CHUNK[:chunk]) + (CHUNK[chunk][0] if which else 0)
    return 128 * first, 128 * CHUNK[chunk][which]


A = [lanes(i, 0) for i in range(len(CHUNK))]
B = [lanes(i, 1) for i in range(len(CHUNK))]
FIRST = [sum(PIECE[:i]) for i in range(len(PIECE))]


def kernel(
    rt_hbm, ds_hbm, dl_hbm, g_hbm, c_hbm, out,
    rt, ds, dl, g, c,
    sb, rb, tb, mb, sq, lhs, rhs, part, cb, red, yb, kb,
    in_sem, s1_send, s1_recv, s2_send, s2_recv,
    za_s, za_r, xa_s, xa_r, xb_s, xb_r, zb_s, zb_r,
    cx_s, cx_r, yx_s, yx_r,
):
    loads = [
        pltpu.make_async_copy(src, dst, in_sem.at[i])
        for i, (src, dst) in enumerate(((c_hbm, c), (rt_hbm, rt), (g_hbm, g), (ds_hbm, ds), (dl_hbm, dl)))
    ]
    for load in loads:
        load.start()
    r = lax.axis_index("trow")
    m = lax.axis_index("mode")
    z, x = r // NX, r % NX
    y, core = m // NCORE, m % NCORE

    def at_z(d):
        return (z + d + NZ) % NZ

    def at_x(d):
        return (x + d + NX) % NX

    def trow_dev(zz, xx):
        return {"trow": zz * NX + xx, "mode": m}

    bar = pltpu.get_barrier_semaphore()

    def greet_trow(j, _):
        pl.semaphore_signal(bar, inc=1, device_id={"trow": (r + 1 + j) % NR, "mode": m}, device_id_type=MESH)
        return 0

    def greet_mode(j, _):
        pl.semaphore_signal(bar, inc=1, device_id={"trow": r, "mode": (m + 1 + j) % NMODE}, device_id_type=MESH)
        return 0

    lax.fori_loop(0, NR - 1, greet_trow, 0)
    lax.fori_loop(0, NMODE - 1, greet_mode, 0)

    loads[0].wait()
    for p in range(2):
        for k in range(2):
            for n in range(8):
                rhs[z, p, x, pl.ds(16 * k, 16), pl.ds(128 * n, 128)] = c[p, k, n]

    def fill():
        loads[1].wait()
        loads[2].wait()

        def one(q, _):
            for i in range(2):
                t = rt[2 * q + i]
                for p in range(2):
                    for o in range(2):
                        sb[q, p, i, o] = g[p, o, t]
            return 0

        lax.fori_loop(0, NR, one, 0)
        rb[r] = sb[r]

    pl.semaphore_wait(bar, NR - 1 + NMODE - 1)

    sent = []

    def block(zz, xx, lanes, half):
        h = slice(None) if half is None else half
        return rhs.at[zz, h, slice(None) if xx is None else xx, :, pl.ds(*lanes)]

    def push(zz, xx, lanes, half, ssem, rsem, dev):
        ref = block(zz, xx, lanes, half)
        d = pltpu.make_async_remote_copy(ref, ref, ssem, rsem, device_id=dev, device_id_type=MESH)
        d.start()
        sent.append(d)

    def landed(zz, xx, lanes, half, rsem):
        ref = block(zz, xx, lanes, half)
        pltpu.make_async_copy(ref, ref, rsem).wait()

    up, down = trow_dev(at_z(1), x), trow_dev(at_z(-1), x)
    right, left = trow_dev(z, at_x(1)), trow_dev(z, at_x(-1))

    def z_send(t, xx, lanes, ssem, rsem):
        lo, hi = (None, None) if t < 4 else (0, 1)
        push(at_z(-(t - 1)), xx, lanes, lo, ssem.at[0, t - 1], rsem.at[0, t - 1], up)
        push(at_z(t - 1), xx, lanes, hi, ssem.at[1, t - 1], rsem.at[1, t - 1], down)

    def z_wait(t, xx, lanes, rsem):
        lo, hi = (None, None) if t < 4 else (0, 1)
        landed(at_z(-t), xx, lanes, lo, rsem.at[0, t - 1])
        landed(at_z(t), xx, lanes, hi, rsem.at[1, t - 1])

    def x_send(d, lanes, ssem, rsem):
        push(at_z(d), x, lanes, None, ssem.at[0], rsem.at[0], right)
        push(at_z(d), x, lanes, None, ssem.at[1], rsem.at[1], left)

    def x_forward(d, lanes, ssem, rsem):
        zz = at_z(d)
        landed(zz, at_x(-1), lanes, None, rsem.at[0])
        push(zz, at_x(-1), lanes, 0, ssem.at[2], rsem.at[2], right)
        landed(zz, at_x(1), lanes, None, rsem.at[1])
        push(zz, at_x(1), lanes, 1, ssem.at[3], rsem.at[3], left)

    def x_last(d, lanes, rsem):
        zz = at_z(d)
        landed(zz, at_x(2), lanes, 0, rsem.at[2])
        landed(zz, at_x(2), lanes, 1, rsem.at[3])

    def za(ch):
        return za_s.at[ch], za_r.at[ch]

    def xa(ch, d):
        return xa_s.at[ch, d % NZ], xa_r.at[ch, d % NZ]

    def hop(ch, t):
        if t > 0:
            z_wait(t, x, A[ch], za(ch)[1])
        if t < 4:
            z_send(t + 1, x, A[ch], *za(ch))
        for d in {0: (0,), 4: (4,)}.get(t, (-t, t)):
            x_send(d, A[ch], *xa(ch, d))

    def forward(ch, t):
        for d in {0: (0,), 4: (4,)}.get(t, (-t, t)):
            x_forward(d, A[ch], *xa(ch, d))

    def last(ch):
        for d in range(NZ):
            x_last(d, A[ch], xa(ch, d)[1])

    def x_first(ch, t):
        xb = (xb_s.at[ch], xb_r.at[ch])
        zb = (zb_s.at[ch], zb_r.at[ch])
        if t == 0:
            x_send(0, B[ch], *xb)
        if t == 1:
            x_forward(0, B[ch], *xb)
        if t == 2:
            x_last(0, B[ch], xb[1])
        if t >= 3:
            z_wait(t - 2, None, B[ch], zb[1])
        if 2 <= t <= 5:
            z_send(t - 1, None, B[ch], *zb)

    def mirror_send(d, e):
        q = at_z(d) * NX + at_x(e)
        pltpu.make_async_remote_copy(
            sb.at[q], rb.at[r], s1_send.at[0], s1_recv.at[r],
            device_id={"trow": q, "mode": m}, device_id_type=MESH,
        ).start()

    lane_group = lax.broadcasted_iota(jnp.int32, (16, 128), 1) // 16

    def mirror_regroup(d):
        kg = at_z(-d)
        for e in range(NX):
            if d == 0 and e == 0:
                continue
            q = kg * NX + at_x(-e)
            pltpu.make_async_copy(rb.at[q], rb.at[q], s1_recv.at[q]).wait()

        def one(ps, _):
            p, s = ps // 2, ps % 2
            tiles = [rb[kg * NX + k // 2, p, s, k % 2].astype(F32) for k in range(8)]
            for bit in (1, 2, 4):
                has = (lane_group // bit) % 2 == 1
                new = list(tiles)
                for k in range(8):
                    if k & bit:
                        continue
                    a, b = tiles[k], tiles[k + bit]
                    new[k] = jnp.where(has, pltpu.roll(b, 16 * bit, 1), a)
                    new[k + bit] = jnp.where(has, b, pltpu.roll(a, 128 - 16 * bit, 1))
                tiles = new
            for j in range(8):
                tb[kg, j, p, s] = tiles[j].astype(BF)
            return 0

        for ps in range(4):
            one(ps, 0)

        def send(j, _):
            to = (m + 1 + j) % NMODE
            pltpu.make_async_remote_copy(
                tb.at[kg, to], mb.at[kg, m], s2_send.at[0], s2_recv.at[kg, m],
                device_id={"trow": r, "mode": to}, device_id_type=MESH,
            ).start()
            return 0

        lax.fori_loop(0, NMODE - 1, send, 0)
        mb[kg, m] = tb[kg, m]

    def sigma(d):
        kg = at_z(-d)

        def arrive(j, _):
            q = (m + 1 + j) % NMODE
            pltpu.make_async_copy(mb.at[kg, q], mb.at[kg, q], s2_recv.at[kg, q]).wait()
            return 0

        lax.fori_loop(0, NMODE - 1, arrive, 0)
        base = pl.multiple_of(kg * 256, 256)
        for s in range(2):
            hr = mb[kg, :, 0, s].reshape(128, 128).astype(F32)
            hi = mb[kg, :, 1, s].reshape(128, 128).astype(F32)
            qr, qi = sq[kg, s, 0], sq[kg, s, 1]
            sr = qr * hr - qi * hi
            si = qr * hi + qi * hr
            lo, hi_lanes = pl.ds(base, 128), pl.ds(base + 128, 128)
            lhs[pl.ds(128 * s, 128), lo] = sr.astype(BF)
            lhs[pl.ds(128 * s, 128), hi_lanes] = (-si).astype(BF)
            lhs[pl.ds(256 + 128 * s, 128), lo] = si.astype(BF)
            lhs[pl.ds(256 + 128 * s, 128), hi_lanes] = sr.astype(BF)

    def squares():
        loads[3].wait()
        loads[4].wait()

        def strengths(k, _):
            t = rt[k]
            row = dl[pl.ds(ds[t], 1), :]
            for s in range(2):
                live = jnp.where(t <= rt[2 * r + s], 1.0, 0.0).astype(F32)
                kb[s, k % 8, pl.ds(k // 8, 1), :] = row * live
            return 0

        lax.fori_loop(0, 64, strengths, 0)
        group8 = lax.broadcasted_iota(jnp.int32, (8, 128), 1) // 16
        for s in range(2):
            rows = jnp.zeros((8, 128), F32)
            for k in range(8):
                turned = pltpu.roll(kb[s, k], (16 * k + 128 - 16 * m) % 128, 1)
                rows = jnp.where(group8 == k, turned, rows)
            kb[s, 8] = rows
        cols = []
        for s in range(2):
            row = dl[pl.ds(ds[rt[2 * r + s]], 1), :]
            cols.append(jnp.broadcast_to(row, (128, 128)).T)

        def one(kg, _):
            for s in range(2):
                coupling = cols[s] * kb[s, 8, pl.ds(kg, 1), :]
                gr = sb[pl.ds(kg * NX, NX), 0, :, s].reshape(128, 128).astype(F32).T
                gi = sb[pl.ds(kg * NX, NX), 1, :, s].reshape(128, 128).astype(F32).T
                sq[kg, s, 0] = (gr * gr - gi * gi) * coupling
                sq[kg, s, 1] = (2.0 * gr * gi) * coupling
            return 0

        lax.fori_loop(0, NZ, one, 0)

    def core_copy(j):
        here = pl.ds(FIRST[j], PIECE[j])
        return pltpu.make_async_remote_copy(
            part.at[:, here, :, 1 - core], cb.at[:, here], cx_s.at[j], cx_r.at[j],
            device_id={"trow": r, "mode": y * NCORE + 1 - core}, device_id_type=MESH,
        )

    def y_copy(j, e):
        here = pl.ds(FIRST[j], PIECE[j])
        to = (y + e) % NY
        return pltpu.make_async_remote_copy(
            red.at[:, here, to], yb.at[e - 1, :, here], yx_s.at[j, e - 1], yx_r.at[j, e - 1],
            device_id={"trow": r, "mode": to * NCORE + core}, device_id_type=MESH,
        )

    def multiply(j):
        n = FIRST[j]
        while n < FIRST[j] + PIECE[j]:
            width = min(2, FIRST[j] + PIECE[j] - n)
            cols = rhs[:, :, :, :, 128 * n : 128 * (n + width)].reshape(2048, 128 * width)
            for h in range(2):
                acc = jnp.dot(lhs[pl.ds(256 * h, 256), :], cols, preferred_element_type=F32)
                for s in range(2):
                    for w in range(width):
                        part[2 * h + s, n + w] = acc[128 * s : 128 * (s + 1), 128 * w : 128 * (w + 1)].reshape(
                            NY, NCORE, 16, 128
                        )
            n += width
        core_copy(j).start()

    def core_sum(j):
        core_copy(j).wait_recv()
        here = pl.ds(FIRST[j], PIECE[j])
        red[:, here] = (part[:, here, :, core] + cb[:, here]).astype(YT)
        for e in (2, 1, 3):
            y_copy(j, e).start()

    def y_sum(j):
        for e in (2, 1, 3):
            y_copy(j, e).wait_recv()
        here = pl.ds(FIRST[j], PIECE[j])
        own = part[:, here, y, core] + cb[:, here, y]
        total = own + (yb[1, :, here].astype(F32) + (yb[0, :, here].astype(F32) + yb[2, :, here].astype(F32)))
        out[:, :, here] = (total * SCALE).reshape(2, 2, PIECE[j], 16, 128)

    hop(1, 0)
    hop(0, 0)
    fill()
    mirror_send(5, 0)
    mirror_send(4, 0)
    mirror_send(1, 2)
    mirror_send(4, 2)
    mirror_send(1, 0)
    mirror_send(1, 1)
    mirror_send(7, 3)
    x_first(0, 0)
    mirror_send(7, 0)
    mirror_send(4, 3)
    mirror_send(3, 1)
    mirror_send(6, 0)
    hop(1, 1)
    hop(0, 1)
    x_first(1, 0)
    mirror_send(0, 1)
    mirror_send(0, 2)
    squares()
    mirror_send(4, 1)
    x_first(1, 1)
    mirror_send(3, 0)
    x_first(0, 1)
    forward(1, 1)
    mirror_send(5, 2)
    mirror_send(3, 3)
    hop(1, 2)
    mirror_send(6, 2)
    forward(0, 0)
    mirror_send(7, 1)
    mirror_send(1, 3)
    mirror_send(7, 2)
    hop(0, 2)
    mirror_regroup(4)
    x_first(1, 2)
    mirror_send(0, 3)
    mirror_send(6, 1)
    mirror_send(2, 0)
    mirror_send(3, 2)
    hop(1, 3)
    mirror_send(2, 2)
    x_first(0, 2)
    mirror_send(5, 1)
    mirror_send(6, 3)
    mirror_regroup(1)
    x_first(1, 3)
    forward(0, 2)
    mirror_regroup(7)
    mirror_send(5, 3)
    sigma(4)
    mirror_regroup(0)
    mirror_send(2, 1)
    forward(1, 2)
    mirror_send(2, 3)
    mirror_regroup(3)
    hop(0, 3)
    x_first(0, 3)
    forward(1, 0)
    forward(1, 3)
    sigma(3)
    hop(1, 4)
    x_first(1, 4)
    forward(0, 1)
    mirror_regroup(6)
    sigma(1)
    mirror_regroup(2)
    sigma(0)
    hop(0, 4)
    x_first(0, 4)
    mirror_regroup(5)
    forward(1, 4)
    sigma(7)
    x_first(1, 5)
    sigma(2)
    forward(0, 3)
    sigma(6)
    last(1)
    forward(0, 4)
    x_first(0, 5)
    x_first(1, 6)
    sigma(5)
    multiply(1)
    x_first(0, 6)
    last(0)
    multiply(0)
    core_sum(1)
    core_sum(0)
    y_sum(1)
    y_sum(0)

    for d in sent:
        d.wait_send()
    all_but_one = sb.at[pl.ds(0, NR - 1)]
    pltpu.make_async_copy(all_but_one, all_but_one, s1_send.at[0]).wait()
    all_but_own = tb.at[:, pl.ds(0, NMODE - 1)]
    pltpu.make_async_copy(all_but_own, all_but_own, s2_send.at[0]).wait()
    for j in range(len(PIECE)):
        core_copy(j).wait_send()
        for e in (2, 1, 3):
            y_copy(j, e).wait_send()


def body(g_hist, new_cols, row_time, drive_step, drive_levels):
    hbm = pl.BlockSpec(memory_space=pltpu.HBM)
    vmem = pl.BlockSpec(memory_space=pltpu.VMEM)
    dma = pltpu.SemaphoreType.DMA
    return pl.pallas_call(
        kernel,
        out_shape=jax.ShapeDtypeStruct((2, 2, 8, 16, 128), F32),
        in_specs=[hbm] * 5,
        out_specs=vmem,
        scratch_shapes=[
            pltpu.SMEM((64,), jnp.int32),
            pltpu.SMEM((64,), jnp.int32),
            pltpu.VMEM((16, 128), F32),
            pltpu.VMEM((2, 2, 64, 16, 128), BF),
            pltpu.VMEM((2, 2, 8, 16, 128), BF),
            pltpu.VMEM((NR, 2, 2, 2, 16, 128), BF),
            pltpu.VMEM((NR, 2, 2, 2, 16, 128), BF),
            pltpu.VMEM((NZ, NMODE, 2, 2, 16, 128), BF),
            pltpu.VMEM((NZ, NMODE, 2, 2, 16, 128), BF),
            pltpu.VMEM((NZ, 2, 2, 128, 128), F32),
            pltpu.VMEM((512, 2048), BF),
            pltpu.VMEM((NZ, 2, NX, 32, 1024), BF),
            pltpu.VMEM((4, 8, NY, NCORE, 16, 128), F32),
            pltpu.VMEM((4, 8, NY, 16, 128), F32),
            pltpu.VMEM((4, 8, NY, 16, 128), YT),
            pltpu.VMEM((3, 4, 8, 16, 128), YT),
            pltpu.VMEM((2, 9, 8, 128), F32),
            dma((5,)), dma((1,)), dma((NR,)), dma((1,)), dma((NZ, NMODE)),
            dma((len(CHUNK), 2, 4)), dma((len(CHUNK), 2, 4)), dma((len(CHUNK), NZ, 4)), dma((len(CHUNK), NZ, 4)),
            dma((len(CHUNK), 4)), dma((len(CHUNK), 4)), dma((len(CHUNK), 2, 4)), dma((len(CHUNK), 2, 4)),
            dma((len(PIECE),)), dma((len(PIECE),)), dma((len(PIECE), 3)), dma((len(PIECE), 3)),
        ],
        compiler_params=pltpu.CompilerParams(
            collective_id=0, has_side_effects=True, vmem_limit_bytes=58 * 1024 * 1024
        ),
        cost_estimate=pl.CostEstimate(flops=2147483648, bytes_accessed=1600000, transcendentals=0),
    )(row_time, drive_step, drive_levels, g_hist, new_cols)


def solution(mesh):
    placed = (
        P(None, "trow", None, "mode", None),
        P(None, "trow", None, "mode", None),
        P(),
        P(),
        P(),
    )
    return jax.shard_map(
        body,
        mesh=mesh,
        in_specs=placed,
        out_specs=P(None, "trow", None, "mode", None),
        check_vma=False,
    )
```

```python
import jax
import jax.numpy as jnp
from jax import lax
from jax.experimental import pallas as pl
from jax.experimental.pallas import tpu as pltpu
from jax.sharding import PartitionSpec as P

NZ, NX, NY, NCORE = 8, 4, 4, 2
NR, NMODE = NZ * NX, NY * NCORE
BF, F32 = jnp.bfloat16, jnp.float32
MESH = pl.DeviceIdType.MESH

CHUNK = ((3, 1), (3, 1))
PIECE = (2, 2, 2, 2)
YT = BF

SCALE = 8.0 / 64


def blocks(chunk, which):
    first = sum(a + b for a, b in CHUNK[:chunk]) + (CHUNK[chunk][0] if which else 0)
    return first, CHUNK[chunk][which]


A = [blocks(i, 0) for i in range(len(CHUNK))]
B = [blocks(i, 1) for i in range(len(CHUNK))]
FIRST = [sum(PIECE[:i]) for i in range(len(PIECE))]


def kernel(
    rt_hbm, ds_hbm, dl_hbm, g_hbm, c_hbm, out,
    rt, ds, dl, g,
    sb, rb, tb, mb, sq, lhs, rhs, part, cb, red, yb, kb,
    in_sem, s1_send, s1_recv, s2_send, s2_recv,
    za_s, za_r, xa_s, xa_r, xb_s, xb_r, zb_s, zb_r,
    cx_s, cx_r, yx_s, yx_r,
):
    r = lax.axis_index("trow")
    m = lax.axis_index("mode")
    z, x = r // NX, r % NX
    y, core = m // NCORE, m % NCORE
    loads = [
        pltpu.make_async_copy(src, dst, in_sem.at[i])
        for i, (src, dst) in enumerate(
            ((g_hbm, g), (rt_hbm, rt), (c_hbm, rhs.at[z, :, x]), (ds_hbm, ds), (dl_hbm, dl))
        )
    ]
    for load in loads:
        load.start()

    def at_z(d):
        return (z + d + NZ) % NZ

    def at_x(d):
        return (x + d + NX) % NX

    def trow_dev(zz, xx):
        return {"trow": zz * NX + xx, "mode": m}

    bar = pltpu.get_barrier_semaphore()

    def greet_trow(j, _):
        pl.semaphore_signal(bar, inc=1, device_id={"trow": (r + 1 + j) % NR, "mode": m}, device_id_type=MESH)
        return 0

    def greet_mode(j, _):
        pl.semaphore_signal(bar, inc=1, device_id={"trow": r, "mode": (m + 1 + j) % NMODE}, device_id_type=MESH)
        return 0

    lax.fori_loop(0, NR - 1, greet_trow, 0)
    lax.fori_loop(0, NMODE - 1, greet_mode, 0)

    def fill():
        for load in loads[:3]:
            load.wait()

        def one(q, _):
            for i in range(2):
                t = rt[2 * q + i]
                for p in range(2):
                    for o in range(2):
                        sb[q, p, i, o] = g[p, o, t]
            return 0

        lax.fori_loop(0, NR, one, 0)
        rb[r] = sb[r]

    pl.semaphore_wait(bar, NR - 1 + NMODE - 1)

    sent = []

    def block(zz, xx, cols, half):
        h = slice(None) if half is None else half
        return rhs.at[zz, h, slice(None) if xx is None else xx, :, pl.ds(*cols)]

    def push(zz, xx, cols, half, ssem, rsem, dev, own=False):
        dst = block(zz, xx, cols, half)
        src = c_hbm.at[:, :, pl.ds(*cols)] if own else dst
        d = pltpu.make_async_remote_copy(src, dst, ssem, rsem, device_id=dev, device_id_type=MESH)
        d.start()
        sent.append(d)

    def landed(zz, xx, cols, half, rsem):
        ref = block(zz, xx, cols, half)
        pltpu.make_async_copy(ref, ref, rsem).wait()

    up, down = trow_dev(at_z(1), x), trow_dev(at_z(-1), x)
    right, left = trow_dev(z, at_x(1)), trow_dev(z, at_x(-1))

    def z_send(t, xx, cols, ssem, rsem):
        lo, hi = (None, None) if t < 4 else (0, 1)
        own = t == 1 and xx is not None
        push(at_z(-(t - 1)), xx, cols, lo, ssem.at[0, t - 1], rsem.at[0, t - 1], up, own)
        push(at_z(t - 1), xx, cols, hi, ssem.at[1, t - 1], rsem.at[1, t - 1], down, own)

    def z_wait(t, xx, cols, rsem):
        lo, hi = (None, None) if t < 4 else (0, 1)
        landed(at_z(-t), xx, cols, lo, rsem.at[0, t - 1])
        landed(at_z(t), xx, cols, hi, rsem.at[1, t - 1])

    def x_send(d, cols, ssem, rsem):
        push(at_z(d), x, cols, None, ssem.at[0], rsem.at[0], right, d == 0)
        push(at_z(d), x, cols, None, ssem.at[1], rsem.at[1], left, d == 0)

    def x_forward(d, cols, ssem, rsem):
        zz = at_z(d)
        landed(zz, at_x(-1), cols, None, rsem.at[0])
        push(zz, at_x(-1), cols, 0, ssem.at[2], rsem.at[2], right)
        landed(zz, at_x(1), cols, None, rsem.at[1])
        push(zz, at_x(1), cols, 1, ssem.at[3], rsem.at[3], left)

    def x_last(d, cols, rsem):
        zz = at_z(d)
        landed(zz, at_x(2), cols, 0, rsem.at[2])
        landed(zz, at_x(2), cols, 1, rsem.at[3])

    def za(ch):
        return za_s.at[ch], za_r.at[ch]

    def xa(ch, d):
        return xa_s.at[ch, d % NZ], xa_r.at[ch, d % NZ]

    def hop(ch, t):
        if t > 0:
            z_wait(t, x, A[ch], za(ch)[1])
        if t < 4:
            z_send(t + 1, x, A[ch], *za(ch))
        for d in {0: (0,), 4: (4,)}.get(t, (-t, t)):
            x_send(d, A[ch], *xa(ch, d))

    def forward(ch, t):
        for d in {0: (0,), 4: (4,)}.get(t, (-t, t)):
            x_forward(d, A[ch], *xa(ch, d))

    def last(ch):
        for d in range(NZ):
            x_last(d, A[ch], xa(ch, d)[1])

    def x_first(ch, t):
        xb = (xb_s.at[ch], xb_r.at[ch])
        zb = (zb_s.at[ch], zb_r.at[ch])
        if t == 0:
            x_send(0, B[ch], *xb)
        if t == 1:
            x_forward(0, B[ch], *xb)
        if t == 2:
            x_last(0, B[ch], xb[1])
        if t >= 3:
            z_wait(t - 2, None, B[ch], zb[1])
        if 2 <= t <= 5:
            z_send(t - 1, None, B[ch], *zb)

    def mirror_send(d, e):
        q = at_z(d) * NX + at_x(e)
        pltpu.make_async_remote_copy(
            sb.at[q], rb.at[r], s1_send.at[0], s1_recv.at[r],
            device_id={"trow": q, "mode": m}, device_id_type=MESH,
        ).start()

    lane_group = lax.broadcasted_iota(jnp.int32, (16, 128), 1) // 16

    def mirror_regroup(d):
        kg = at_z(-d)
        for e in range(NX):
            if d == 0 and e == 0:
                continue
            q = kg * NX + at_x(-e)
            pltpu.make_async_copy(rb.at[q], rb.at[q], s1_recv.at[q]).wait()

        def one(ps, _):
            p, s = ps // 2, ps % 2
            tiles = [rb[kg * NX + k // 2, p, s, k % 2] for k in range(8)]
            for bit in (1, 2, 4):
                has = (lane_group // bit) % 2 == 1
                new = list(tiles)
                for k in range(8):
                    if k & bit:
                        continue
                    a, b = tiles[k], tiles[k + bit]
                    new[k] = jnp.where(has, pltpu.roll(b, 16 * bit, 1), a)
                    new[k + bit] = jnp.where(has, b, pltpu.roll(a, 128 - 16 * bit, 1))
                tiles = new
            for j in range(8):
                tb[kg, j, p, s] = tiles[j]
            return 0

        for ps in range(4):
            one(ps, 0)

        def send(j, _):
            to = (m + 1 + j) % NMODE
            pltpu.make_async_remote_copy(
                tb.at[kg, to], mb.at[kg, m], s2_send.at[0], s2_recv.at[kg, m],
                device_id={"trow": r, "mode": to}, device_id_type=MESH,
            ).start()
            return 0

        lax.fori_loop(0, NMODE - 1, send, 0)
        mb[kg, m] = tb[kg, m]

    def sigma(d):
        kg = at_z(-d)

        def arrive(j, _):
            q = (m + 1 + j) % NMODE
            pltpu.make_async_copy(mb.at[kg, q], mb.at[kg, q], s2_recv.at[kg, q]).wait()
            return 0

        lax.fori_loop(0, NMODE - 1, arrive, 0)
        base = pl.multiple_of(kg * 256, 256)
        for s in range(2):
            hr = mb[kg, :, 0, s].reshape(128, 128).astype(F32)
            hi = mb[kg, :, 1, s].reshape(128, 128).astype(F32)
            qr, qi = sq[kg, s, 0], sq[kg, s, 1]
            sr = qr * hr - qi * hi
            si = qr * hi + qi * hr
            lo, hi_lanes = pl.ds(base, 128), pl.ds(base + 128, 128)
            lhs[pl.ds(128 * s, 128), lo] = sr.astype(BF)
            lhs[pl.ds(128 * s, 128), hi_lanes] = (-si).astype(BF)
            lhs[pl.ds(256 + 128 * s, 128), lo] = si.astype(BF)
            lhs[pl.ds(256 + 128 * s, 128), hi_lanes] = sr.astype(BF)

    def squares():
        loads[3].wait()
        loads[4].wait()

        def strengths(k, _):
            t = rt[k]
            row = dl[pl.ds(ds[t], 1), :]
            for s in range(2):
                live = jnp.where(t <= rt[2 * r + s], 1.0, 0.0).astype(F32)
                kb[s, k % 8, pl.ds(k // 8, 1), :] = row * live
            return 0

        lax.fori_loop(0, 64, strengths, 0)
        group8 = lax.broadcasted_iota(jnp.int32, (8, 128), 1) // 16
        for s in range(2):
            rows = jnp.zeros((8, 128), F32)
            for k in range(8):
                turned = pltpu.roll(kb[s, k], (16 * k + 128 - 16 * m) % 128, 1)
                rows = jnp.where(group8 == k, turned, rows)
            kb[s, 8] = rows
        cols = []
        for s in range(2):
            row = dl[pl.ds(ds[rt[2 * r + s]], 1), :]
            cols.append(jnp.broadcast_to(row, (128, 128)).T)

        def one(kg, _):
            for s in range(2):
                coupling = cols[s] * kb[s, 8, pl.ds(kg, 1), :]
                gr = sb[pl.ds(kg * NX, NX), 0, :, s].reshape(128, 128).astype(F32).T
                gi = sb[pl.ds(kg * NX, NX), 1, :, s].reshape(128, 128).astype(F32).T
                sq[kg, s, 0] = (gr * gr - gi * gi) * coupling
                sq[kg, s, 1] = (2.0 * gr * gi) * coupling
            return 0

        lax.fori_loop(0, NZ, one, 0)

    def core_copy(j):
        here = pl.ds(FIRST[j], PIECE[j])
        return pltpu.make_async_remote_copy(
            part.at[:, here, :, 1 - core], cb.at[:, here], cx_s.at[j], cx_r.at[j],
            device_id={"trow": r, "mode": y * NCORE + 1 - core}, device_id_type=MESH,
        )

    def y_copy(j, e):
        here = pl.ds(FIRST[j], PIECE[j])
        to = (y + e) % NY
        return pltpu.make_async_remote_copy(
            red.at[:, here, to], yb.at[e - 1, :, here], yx_s.at[j, e - 1], yx_r.at[j, e - 1],
            device_id={"trow": r, "mode": to * NCORE + core}, device_id_type=MESH,
        )

    def multiply(j):
        def product(n, width):
            cols = jnp.concatenate([rhs[:, :, :, :, n + w].reshape(2048, 128) for w in range(width)], axis=1)

            def half(h, _):
                rows = lhs[pl.ds(pl.multiple_of(256 * h, 256), 256), :]
                acc = jnp.dot(rows, cols, preferred_element_type=F32)
                for s in range(2):
                    for w in range(width):
                        part[2 * h + s, n + w] = acc[128 * s : 128 * (s + 1), 128 * w : 128 * (w + 1)].reshape(
                            NY, NCORE, 16, 128
                        )
                return 0

            for h in range(2):
                half(h, 0)

        def pair(i, _):
            product(FIRST[j] + 2 * i, 2)
            return 0

        lax.fori_loop(0, PIECE[j] // 2, pair, 0)
        if PIECE[j] % 2:
            product(FIRST[j] + PIECE[j] - 1, 1)
        core_copy(j).start()

    def core_sum(j):
        core_copy(j).wait_recv()
        here = pl.ds(FIRST[j], PIECE[j])
        red[:, here] = (part[:, here, :, core] + cb[:, here]).astype(YT)
        for e in (2, 1, 3):
            y_copy(j, e).start()

    def y_sum(j):
        for e in (2, 1, 3):
            y_copy(j, e).wait_recv()
        here = pl.ds(FIRST[j], PIECE[j])
        own = part[:, here, y, core] + cb[:, here, y]
        total = own + (yb[1, :, here].astype(F32) + (yb[0, :, here].astype(F32) + yb[2, :, here].astype(F32)))
        out[:, :, here] = (total * SCALE).reshape(2, 2, PIECE[j], 16, 128)

    hop(1, 0)
    hop(0, 0)
    fill()
    mirror_send(4, 0)
    mirror_send(4, 2)
    x_first(0, 0)
    forward(1, 0)
    mirror_send(4, 3)
    x_first(1, 0)
    mirror_send(2, 3)
    mirror_send(6, 1)
    mirror_send(4, 1)
    hop(0, 1)
    hop(1, 1)
    x_first(0, 1)
    mirror_send(3, 2)
    mirror_send(5, 2)
    mirror_send(0, 1)
    x_first(1, 1)
    mirror_send(5, 3)
    mirror_send(0, 2)
    mirror_send(5, 0)
    mirror_send(3, 1)
    mirror_send(0, 3)
    hop(0, 2)
    squares()
    mirror_regroup(4)
    mirror_send(1, 0)
    mirror_send(1, 1)
    mirror_send(6, 2)
    mirror_send(1, 2)
    mirror_send(3, 0)
    mirror_send(2, 0)
    x_first(0, 2)
    mirror_send(1, 3)
    mirror_send(6, 3)
    mirror_regroup(0)
    forward(0, 2)
    hop(1, 2)
    mirror_send(3, 3)
    mirror_send(5, 1)
    forward(1, 2)
    hop(0, 3)
    x_first(1, 2)
    mirror_send(6, 0)
    x_first(0, 3)
    mirror_send(7, 0)
    mirror_send(7, 3)
    hop(1, 3)
    mirror_send(7, 1)
    mirror_send(2, 2)
    mirror_send(7, 2)
    mirror_regroup(5)
    mirror_regroup(1)
    mirror_send(2, 1)
    hop(0, 4)
    mirror_regroup(3)
    forward(0, 1)
    mirror_regroup(6)
    forward(0, 3)
    x_first(1, 3)
    x_first(0, 4)
    hop(1, 4)
    forward(0, 0)
    sigma(0)
    sigma(1)
    forward(1, 3)
    mirror_regroup(7)
    mirror_regroup(2)
    x_first(1, 4)
    sigma(3)
    forward(0, 4)
    sigma(6)
    forward(1, 1)
    x_first(0, 5)
    forward(1, 4)
    sigma(4)
    sigma(7)
    sigma(5)
    last(0)
    x_first(1, 5)
    sigma(2)
    x_first(0, 6)
    multiply(0)
    multiply(1)
    last(1)
    x_first(1, 6)
    multiply(3)
    core_sum(0)
    multiply(2)
    core_sum(1)
    core_sum(3)
    core_sum(2)
    y_sum(3)
    y_sum(0)
    y_sum(1)
    y_sum(2)

    for d in sent:
        d.wait_send()
    all_but_one = sb.at[pl.ds(0, NR - 1)]
    pltpu.make_async_copy(all_but_one, all_but_one, s1_send.at[0]).wait()
    all_but_own = tb.at[:, pl.ds(0, NMODE - 1)]
    pltpu.make_async_copy(all_but_own, all_but_own, s2_send.at[0]).wait()
    for j in range(len(PIECE)):
        core_copy(j).wait_send()
        for e in (2, 1, 3):
            y_copy(j, e).wait_send()


def body(g_hist, new_cols, row_time, drive_step, drive_levels):
    hbm = pl.BlockSpec(memory_space=pltpu.HBM)
    operands = [
        pltpu.with_memory_space_constraint(v, pltpu.HBM)
        for v in (row_time, drive_step, drive_levels, g_hist, new_cols)
    ]
    vmem = pl.BlockSpec(memory_space=pltpu.VMEM)
    dma = pltpu.SemaphoreType.DMA
    return pl.pallas_call(
        kernel,
        out_shape=jax.ShapeDtypeStruct((2, 2, 8, 16, 128), F32),
        in_specs=[hbm] * 5,
        out_specs=vmem,
        scratch_shapes=[
            pltpu.SMEM((64,), jnp.int32),
            pltpu.SMEM((64,), jnp.int32),
            pltpu.VMEM((16, 128), F32),
            pltpu.VMEM((2, 2, 64, 16, 128), BF),
            pltpu.VMEM((NR, 2, 2, 2, 16, 128), BF),
            pltpu.VMEM((NR, 2, 2, 2, 16, 128), BF),
            pltpu.VMEM((NZ, NMODE, 2, 2, 16, 128), BF),
            pltpu.VMEM((NZ, NMODE, 2, 2, 16, 128), BF),
            pltpu.VMEM((NZ, 2, 2, 128, 128), F32),
            pltpu.VMEM((512, 2048), BF),
            pltpu.VMEM((NZ, 2, NX, 2, 8, 16, 128), BF),
            pltpu.VMEM((4, 8, NY, NCORE, 16, 128), F32),
            pltpu.VMEM((4, 8, NY, 16, 128), F32),
            pltpu.VMEM((4, 8, NY, 16, 128), YT),
            pltpu.VMEM((3, 4, 8, 16, 128), YT),
            pltpu.VMEM((2, 9, 8, 128), F32),
            dma((5,)), dma((1,)), dma((NR,)), dma((1,)), dma((NZ, NMODE)),
            dma((len(CHUNK), 2, 4)), dma((len(CHUNK), 2, 4)), dma((len(CHUNK), NZ, 4)), dma((len(CHUNK), NZ, 4)),
            dma((len(CHUNK), 4)), dma((len(CHUNK), 4)), dma((len(CHUNK), 2, 4)), dma((len(CHUNK), 2, 4)),
            dma((len(PIECE),)), dma((len(PIECE),)), dma((len(PIECE), 3)), dma((len(PIECE), 3)),
        ],
        compiler_params=pltpu.CompilerParams(
            collective_id=0, has_side_effects=True, vmem_limit_bytes=40 * 1024 * 1024
        ),
        cost_estimate=pl.CostEstimate(flops=2147483648, bytes_accessed=1600000, transcendentals=0),
    )(*operands)


def solution(mesh):
    placed = (
        P(None, "trow", None, "mode", None),
        P(None, "trow", None, "mode", None),
        P(),
        P(),
        P(),
    )
    return jax.shard_map(
        body,
        mesh=mesh,
        in_specs=placed,
        out_specs=P(None, "trow", None, "mode", None),
        check_vma=False,
    )
```

```python
import jax
import jax.numpy as jnp
from jax import lax
from jax.experimental import pallas as pl
from jax.experimental.pallas import tpu as pltpu
from jax.sharding import PartitionSpec as P

NZ, NX, NY, NCORE = 8, 4, 4, 2
NR, NMODE = NZ * NX, NY * NCORE
BF, F32 = jnp.bfloat16, jnp.float32
MESH = pl.DeviceIdType.MESH

CHUNK = ((1, 1), (2, 0))
PIECE = (2, 2)

SCALE = 8.0 / 64


def blocks(chunk, which):
    first = sum(a + b for a, b in CHUNK[:chunk]) + (CHUNK[chunk][0] if which else 0)
    return first, CHUNK[chunk][which]


A = [blocks(i, 0) for i in range(len(CHUNK))]
B = [blocks(i, 1) for i in range(len(CHUNK))]
LAST = 0
SUM_ORDER = ((2, 0), (2, 1), (1, 0), (3, 0), (1, 1), (3, 1), (0, 1))
FIRST = [sum(PIECE[:i]) for i in range(len(PIECE))]


def kernel(
    rt_hbm, ds_hbm, dl_hbm, g_hbm, c_hbm, out,
    rt, ds, dl, g,
    sb, rb, tb, mb, sq, lhs, rhs, part, part16, gathered, kb,
    in_sem, s1_send, s1_recv, s2_send, s2_recv,
    za_s, za_r, xa_s, xa_r, xb_s, xb_r, zb_s, zb_r,
    sw_s, sw_r, sg_s, sg_r, sum_s, sum_r,
):
    r = lax.axis_index("trow")
    m = lax.axis_index("mode")
    z, x = r // NX, r % NX
    y, core = m // NCORE, m % NCORE
    loads = [
        pltpu.make_async_copy(src, dst, in_sem.at[i])
        for i, (src, dst) in enumerate(
            ((g_hbm, g), (rt_hbm, rt), (c_hbm.at[:, :, pl.ds(4 * core, 4)], rhs.at[z, core, :, x]), (ds_hbm, ds), (dl_hbm, dl))
        )
    ]
    for load in loads:
        load.start()

    def at_z(d):
        return (z + d + NZ) % NZ

    def at_x(d):
        return (x + d + NX) % NX

    def trow_dev(zz, xx):
        return {"trow": zz * NX + xx, "mode": m}

    bar = pltpu.get_barrier_semaphore()

    def greet_trow(j, _):
        pl.semaphore_signal(bar, inc=1, device_id={"trow": (r + 1 + j) % NR, "mode": m}, device_id_type=MESH)
        return 0

    def greet_mode(j, _):
        pl.semaphore_signal(bar, inc=1, device_id={"trow": r, "mode": (m + 1 + j) % NMODE}, device_id_type=MESH)
        return 0

    lax.fori_loop(0, NR - 1, greet_trow, 0)
    lax.fori_loop(0, NMODE - 1, greet_mode, 0)

    def fill():
        for load in loads[:2]:
            load.wait()

        def one(q, _):
            for i in range(2):
                t = rt[2 * q + i]
                for p in range(2):
                    for o in range(2):
                        sb[q, p, i, o] = g[p, o, t]
            return 0

        lax.fori_loop(0, NR, one, 0)
        rb[r] = sb[r]

    pl.semaphore_wait(bar, NR - 1 + NMODE - 1)

    swap = pltpu.make_async_remote_copy(
        c_hbm.at[:, :, pl.ds(4 * (1 - core), 4)], rhs.at[z, core, :, x], sw_s.at[0], sw_r.at[0],
        device_id={"trow": r, "mode": y * NCORE + 1 - core}, device_id_type=MESH,
    )
    swap.start()

    def swapped():
        loads[2].wait()
        swap.wait()

    sent = []

    def block(zz, xx, cols, half):
        h = slice(None) if half is None else half
        return rhs.at[zz, :, h, slice(None) if xx is None else xx, :, pl.ds(*cols)]

    def push(zz, xx, cols, half, ssem, rsem, dev):
        ref = block(zz, xx, cols, half)
        d = pltpu.make_async_remote_copy(ref, ref, ssem, rsem, device_id=dev, device_id_type=MESH)
        d.start()
        sent.append(d)

    def landed(zz, xx, cols, half, rsem):
        ref = block(zz, xx, cols, half)
        pltpu.make_async_copy(ref, ref, rsem).wait()

    up, down = trow_dev(at_z(1), x), trow_dev(at_z(-1), x)
    right, left = trow_dev(z, at_x(1)), trow_dev(z, at_x(-1))

    def z_send(t, xx, cols, ssem, rsem):
        lo, hi = (None, None) if t < 4 else (0, 1)
        push(at_z(-(t - 1)), xx, cols, lo, ssem.at[0, t - 1], rsem.at[0, t - 1], up)
        push(at_z(t - 1), xx, cols, hi, ssem.at[1, t - 1], rsem.at[1, t - 1], down)

    def z_wait(t, xx, cols, rsem):
        lo, hi = (None, None) if t < 4 else (0, 1)
        landed(at_z(-t), xx, cols, lo, rsem.at[0, t - 1])
        landed(at_z(t), xx, cols, hi, rsem.at[1, t - 1])

    def x_send(d, cols, ssem, rsem):
        push(at_z(d), x, cols, None, ssem.at[0], rsem.at[0], right)
        push(at_z(d), x, cols, None, ssem.at[1], rsem.at[1], left)

    def x_forward(d, cols, ssem, rsem):
        zz = at_z(d)
        landed(zz, at_x(-1), cols, None, rsem.at[0])
        push(zz, at_x(-1), cols, 0, ssem.at[2], rsem.at[2], right)
        landed(zz, at_x(1), cols, None, rsem.at[1])
        push(zz, at_x(1), cols, 1, ssem.at[3], rsem.at[3], left)

    def x_last(d, cols, rsem):
        zz = at_z(d)
        landed(zz, at_x(2), cols, 0, rsem.at[2])
        landed(zz, at_x(2), cols, 1, rsem.at[3])

    def za(ch):
        return za_s.at[ch], za_r.at[ch]

    def xa(ch, d):
        return xa_s.at[ch, d % NZ], xa_r.at[ch, d % NZ]

    def hop(ch, t):
        if t > 0:
            z_wait(t, x, A[ch], za(ch)[1])
        if t < 4:
            z_send(t + 1, x, A[ch], *za(ch))
        for d in {0: (0,), 4: (4,)}.get(t, (-t, t)):
            x_send(d, A[ch], *xa(ch, d))

    def forward(ch, t):
        for d in {0: (0,), 4: (4,)}.get(t, (-t, t)):
            x_forward(d, A[ch], *xa(ch, d))

    def last(ch):
        for d in range(NZ):
            x_last(d, A[ch], xa(ch, d)[1])

    def x_first(ch, t):
        xb = (xb_s.at[ch], xb_r.at[ch])
        zb = (zb_s.at[ch], zb_r.at[ch])
        if t == 0:
            x_send(0, B[ch], *xb)
        if t == 1:
            x_forward(0, B[ch], *xb)
        if t == 2:
            x_last(0, B[ch], xb[1])
        if t >= 3:
            z_wait(t - 2, None, B[ch], zb[1])
        if 2 <= t <= 5:
            z_send(t - 1, None, B[ch], *zb)

    def mirror_send(d, e):
        q = at_z(d) * NX + at_x(e)
        pltpu.make_async_remote_copy(
            sb.at[q], rb.at[r], s1_send.at[0], s1_recv.at[r],
            device_id={"trow": q, "mode": m}, device_id_type=MESH,
        ).start()

    lane_group = lax.broadcasted_iota(jnp.int32, (16, 128), 1) // 16

    def mirror_regroup(d):
        kg = at_z(-d)
        for e in range(NX):
            if d == 0 and e == 0:
                continue
            q = kg * NX + at_x(-e)
            pltpu.make_async_copy(rb.at[q], rb.at[q], s1_recv.at[q]).wait()

        def one(ps, _):
            p, s = ps // 2, ps % 2
            tiles = [rb[kg * NX + k // 2, p, s, k % 2] for k in range(8)]
            for bit in (1, 2, 4):
                has = (lane_group // bit) % 2 == 1
                new = list(tiles)
                for k in range(8):
                    if k & bit:
                        continue
                    a, b = tiles[k], tiles[k + bit]
                    new[k] = jnp.where(has, pltpu.roll(b, 16 * bit, 1), a)
                    new[k + bit] = jnp.where(has, b, pltpu.roll(a, 128 - 16 * bit, 1))
                tiles = new
            for j in range(8):
                tb[kg, j, p, s] = tiles[j]
            return 0

        for ps in range(4):
            one(ps, 0)

        def send(j, _):
            to = (m + 1 + j) % NMODE
            pltpu.make_async_remote_copy(
                tb.at[kg, to], mb.at[kg, m], s2_send.at[0], s2_recv.at[kg, m],
                device_id={"trow": r, "mode": to}, device_id_type=MESH,
            ).start()
            return 0

        lax.fori_loop(0, NMODE - 1, send, 0)
        mb[kg, m] = tb[kg, m]

    def sigma(d):
        kg = at_z(-d)

        def arrive(j, _):
            q = (m + 1 + j) % NMODE
            pltpu.make_async_copy(mb.at[kg, q], mb.at[kg, q], s2_recv.at[kg, q]).wait()
            return 0

        lax.fori_loop(0, NMODE - 1, arrive, 0)
        base = pl.multiple_of(kg * 512 + core * 256, 256)
        for s in range(2):
            hr = mb[kg, :, 0, s].reshape(128, 128).astype(F32)
            hi = mb[kg, :, 1, s].reshape(128, 128).astype(F32)
            qr, qi = sq[kg, s, 0], sq[kg, s, 1]
            sr = qr * hr - qi * hi
            si = qr * hi + qi * hr
            lo, hi_lanes = pl.ds(base, 128), pl.ds(base + 128, 128)
            lhs[pl.ds(128 * s, 128), lo] = sr.astype(BF)
            lhs[pl.ds(128 * s, 128), hi_lanes] = (-si).astype(BF)
            lhs[pl.ds(256 + 128 * s, 128), lo] = si.astype(BF)
            lhs[pl.ds(256 + 128 * s, 128), hi_lanes] = sr.astype(BF)

        sigma_copy(d).start()

    def sigma_copy(d):
        here = lhs.at[:, pl.ds(pl.multiple_of(at_z(-d) * 512 + core * 256, 256), 256)]
        return pltpu.make_async_remote_copy(
            here, here, sg_s.at[d], sg_r.at[d],
            device_id={"trow": r, "mode": y * NCORE + 1 - core}, device_id_type=MESH,
        )

    def sigmas_landed():
        for d in range(NZ):
            other = lhs.at[:, pl.ds(pl.multiple_of(at_z(-d) * 512 + (1 - core) * 256, 256), 256)]
            pltpu.make_async_copy(other, other, sg_r.at[d]).wait()

    def squares():
        loads[3].wait()
        loads[4].wait()

        def strengths(k, _):
            t = rt[k]
            row = dl[pl.ds(ds[t], 1), :]
            for s in range(2):
                live = jnp.where(t <= rt[2 * r + s], 1.0, 0.0).astype(F32)
                kb[s, k % 8, pl.ds(k // 8, 1), :] = row * live
            return 0

        lax.fori_loop(0, 64, strengths, 0)
        group8 = lax.broadcasted_iota(jnp.int32, (8, 128), 1) // 16
        for s in range(2):
            rows = jnp.zeros((8, 128), F32)
            for k in range(8):
                turned = pltpu.roll(kb[s, k], (16 * k + 128 - 16 * m) % 128, 1)
                rows = jnp.where(group8 == k, turned, rows)
            kb[s, 8] = rows
        cols = []
        for s in range(2):
            row = dl[pl.ds(ds[rt[2 * r + s]], 1), :]
            cols.append(jnp.broadcast_to(row, (128, 128)).T)

        def one(kg, _):
            for s in range(2):
                coupling = cols[s] * kb[s, 8, pl.ds(kg, 1), :]
                gr = sb[pl.ds(kg * NX, NX), 0, :, s].reshape(128, 128).astype(F32).T
                gi = sb[pl.ds(kg * NX, NX), 1, :, s].reshape(128, 128).astype(F32).T
                sq[kg, s, 0] = (gr * gr - gi * gi) * coupling
                sq[kg, s, 1] = (2.0 * gr * gi) * coupling
            return 0

        lax.fori_loop(0, NZ, one, 0)

    def sum_copy(j, e, other):
        here = pl.ds(FIRST[j], PIECE[j])
        ty, tc = (y + e) % NY, (1 - core if other else core)
        return pltpu.make_async_remote_copy(
            part16.at[:, here, ty, tc], gathered.at[other, e, :, here], sum_s.at[j, other, e], sum_r.at[j, other, e],
            device_id={"trow": r, "mode": ty * NCORE + tc}, device_id_type=MESH,
        )

    def multiply(j):
        def product(n, width):
            cols = jnp.concatenate([rhs[:, :, :, :, :, n + w].reshape(4096, 128) for w in range(width)], axis=1)
            for h in range(2):
                rows = lhs[256 * h : 256 * (h + 1), :]
                acc = jnp.dot(rows, cols, preferred_element_type=F32)
                for s in range(2):
                    for w in range(width):
                        tile = acc[128 * s : 128 * (s + 1), 128 * w : 128 * (w + 1)].reshape(NY, NCORE, 16, 128)
                        part[2 * h + s, n + w] = tile
                        part16[2 * h + s, n + w] = tile.astype(BF)

        for i in range(PIECE[j] // 2):
            product(FIRST[j] + 2 * i, 2)
        if PIECE[j] % 2:
            product(FIRST[j] + PIECE[j] - 1, 1)
        for e, other in SUM_ORDER:
            sum_copy(j, e, other).start()

    def y_sum(j):
        for e, other in SUM_ORDER:
            sum_copy(j, e, other).wait_recv()
        here = pl.ds(FIRST[j], PIECE[j])
        mine = part[:, here, y, core]
        theirs = gathered[1, 0, :, here].astype(F32)
        for e in range(1, NY):
            mine += gathered[0, e, :, here].astype(F32)
            theirs += gathered[1, e, :, here].astype(F32)
        out[:, :, pl.ds(4 * core + FIRST[j], PIECE[j])] = (mine * SCALE).reshape(2, 2, PIECE[j], 16, 128)
        out[:, :, pl.ds(4 * (1 - core) + FIRST[j], PIECE[j])] = (theirs * SCALE).reshape(2, 2, PIECE[j], 16, 128)

    def sums_left(j):
        for e, other in SUM_ORDER:
            sum_copy(j, e, other).wait_send()

    def drain():
        for d in sent:
            d.wait_send()
        all_but_one = sb.at[pl.ds(0, NR - 1)]
        pltpu.make_async_copy(all_but_one, all_but_one, s1_send.at[0]).wait()
        all_but_own = tb.at[:, pl.ds(0, NMODE - 1)]
        pltpu.make_async_copy(all_but_own, all_but_own, s2_send.at[0]).wait()
        for d in range(NZ):
            sigma_copy(d).wait_send()
        for j in range(len(PIECE)):
            if j != LAST:
                sums_left(j)

    fill()
    mirror_send(2, 0)
    mirror_send(7, 0)
    mirror_send(4, 1)
    mirror_send(6, 0)
    mirror_send(1, 0)
    mirror_send(2, 1)
    mirror_send(5, 2)
    mirror_send(7, 2)
    squares()
    mirror_send(6, 2)
    mirror_send(3, 2)
    mirror_send(7, 1)
    swapped()
    mirror_send(7, 3)
    hop(0, 0)
    mirror_send(6, 1)
    mirror_send(0, 3)
    hop(1, 0)
    mirror_send(6, 3)
    mirror_send(3, 3)
    mirror_send(2, 3)
    x_first(0, 0)
    mirror_send(3, 0)
    mirror_send(5, 0)
    mirror_send(2, 2)
    mirror_send(0, 2)
    forward(1, 0)
    mirror_send(1, 2)
    hop(0, 1)
    mirror_send(0, 1)
    x_first(0, 1)
    hop(1, 1)
    mirror_regroup(0)
    x_first(0, 2)
    mirror_regroup(6)
    forward(0, 1)
    mirror_send(5, 3)
    mirror_send(1, 3)
    mirror_send(3, 1)
    hop(1, 2)
    mirror_send(5, 1)
    mirror_regroup(7)
    mirror_regroup(2)
    mirror_send(1, 1)
    sigma(6)
    mirror_send(4, 2)
    mirror_send(4, 3)
    mirror_send(4, 0)
    hop(0, 2)
    mirror_regroup(3)
    sigma(7)
    sigma(0)
    hop(1, 3)
    mirror_regroup(1)
    forward(0, 2)
    mirror_regroup(5)
    sigma(3)
    forward(1, 2)
    x_first(0, 3)
    forward(1, 1)
    mirror_regroup(4)
    hop(1, 4)
    sigma(5)
    hop(0, 3)
    x_first(0, 4)
    hop(0, 4)
    sigma(4)
    forward(1, 4)
    forward(1, 3)
    sigma(2)
    forward(0, 0)
    sigma(1)
    forward(0, 3)
    x_first(0, 5)
    forward(0, 4)
    sigmas_landed()
    last(1)
    multiply(1)
    last(0)
    x_first(0, 6)
    multiply(0)
    y_sum(1)
    drain()
    y_sum(0)

    sums_left(LAST)


def body(g_hist, new_cols, row_time, drive_step, drive_levels):
    hbm = pl.BlockSpec(memory_space=pltpu.HBM)
    operands = [
        pltpu.with_memory_space_constraint(v, pltpu.HBM)
        for v in (row_time, drive_step, drive_levels, g_hist, new_cols)
    ]
    vmem = pl.BlockSpec(memory_space=pltpu.VMEM)
    dma = pltpu.SemaphoreType.DMA
    return pl.pallas_call(
        kernel,
        out_shape=jax.ShapeDtypeStruct((2, 2, 8, 16, 128), F32),
        in_specs=[hbm] * 5,
        out_specs=vmem,
        scratch_shapes=[
            pltpu.SMEM((64,), jnp.int32),
            pltpu.SMEM((64,), jnp.int32),
            pltpu.VMEM((16, 128), F32),
            pltpu.VMEM((2, 2, 64, 16, 128), BF),
            pltpu.VMEM((NR, 2, 2, 2, 16, 128), BF),
            pltpu.VMEM((NR, 2, 2, 2, 16, 128), BF),
            pltpu.VMEM((NZ, NMODE, 2, 2, 16, 128), BF),
            pltpu.VMEM((NZ, NMODE, 2, 2, 16, 128), BF),
            pltpu.VMEM((NZ, 2, 2, 128, 128), F32),
            pltpu.VMEM((512, 4096), BF),
            pltpu.VMEM((NZ, NCORE, 2, NX, 2, 4, 16, 128), BF),
            pltpu.VMEM((4, 4, NY, NCORE, 16, 128), F32),
            pltpu.VMEM((4, 4, NY, NCORE, 16, 128), BF),
            pltpu.VMEM((2, NY, 4, 4, 16, 128), BF),
            pltpu.VMEM((2, 9, 8, 128), F32),
            dma((5,)), dma((1,)), dma((NR,)), dma((1,)), dma((NZ, NMODE)),
            dma((len(CHUNK), 2, 4)), dma((len(CHUNK), 2, 4)), dma((len(CHUNK), NZ, 4)), dma((len(CHUNK), NZ, 4)),
            dma((len(CHUNK), 4)), dma((len(CHUNK), 4)), dma((len(CHUNK), 2, 4)), dma((len(CHUNK), 2, 4)),
            dma((1,)), dma((1,)), dma((NZ,)), dma((NZ,)), dma((len(PIECE), 2, NY)), dma((len(PIECE), 2, NY)),
        ],
        compiler_params=pltpu.CompilerParams(
            collective_id=0, has_side_effects=True, vmem_limit_bytes=40 * 1024 * 1024
        ),
        cost_estimate=pl.CostEstimate(flops=2147483648, bytes_accessed=1600000, transcendentals=0),
    )(*operands)


def solution(mesh):
    placed = (
        P(None, "trow", None, "mode", None),
        P(None, "trow", None, "mode", None),
        P(),
        P(),
        P(),
    )
    return jax.shard_map(
        body,
        mesh=mesh,
        in_specs=placed,
        out_specs=P(None, "trow", None, "mode", None),
        check_vma=False,
    )
```

```python
import jax
import jax.numpy as jnp
from jax import lax
from jax.experimental import pallas as pl
from jax.experimental.pallas import tpu as pltpu
from jax.sharding import PartitionSpec as P

NZ, NX, NY, NCORE = 8, 4, 4, 2
NR, NMODE = NZ * NX, NY * NCORE
BF, F32 = jnp.bfloat16, jnp.float32
MESH = pl.DeviceIdType.MESH

CHUNK = ((4, 0), (3, 1))
PIECE = (2, 2)

SCALE = 8.0 / 64


def blocks(chunk, which):
    first = sum(a + b for a, b in CHUNK[:chunk]) + (CHUNK[chunk][0] if which else 0)
    return first, CHUNK[chunk][which]


A = [blocks(i, 0) for i in range(len(CHUNK))]
B = [blocks(i, 1) for i in range(len(CHUNK))]
LAST = 1
FAR = ((0, 1, 2, 6, 7), (3, 4, 5))
SUM_ORDER = ((2, 0), (2, 1), (1, 0), (3, 0), (1, 1), (3, 1), (0, 1))
FIRST = [sum(PIECE[:i]) for i in range(len(PIECE))]


def kernel(
    rt_hbm, ds_hbm, dl_hbm, g_hbm, c_hbm, out,
    rt, ds, dl, g,
    sb, rb, tb, mb, sq, lhs, rhs, part, part16, gathered, kb,
    in_sem, col_sem, s1_send, s1_recv, s2_send, s2_recv,
    za_s, za_r, xa_s, xa_r, xb_s, xb_r, zb_s, zb_r,
    sw_s, sw_r, sg_s, sg_r, sum_s, sum_r,
):
    r = lax.axis_index("trow")
    m = lax.axis_index("mode")
    z, x = r // NX, r % NX
    y, core = m // NCORE, m % NCORE
    loads = [
        pltpu.make_async_copy(src, dst, in_sem.at[i])
        for i, (src, dst) in enumerate(
            ((g_hbm, g), (rt_hbm, rt), (ds_hbm, ds), (dl_hbm, dl))
        )
    ]
    own_cols = [
        pltpu.make_async_copy(
            c_hbm.at[:, i % 2, 4 * core + i // 2], rhs.at[z, core, :, x, i], col_sem.at[i]
        )
        for i in range(8)
    ]
    for load in loads + own_cols:
        load.start()

    def at_z(d):
        return (z + d + NZ) % NZ

    def at_x(d):
        return (x + d + NX) % NX

    def trow_dev(zz, xx):
        return {"trow": zz * NX + xx, "mode": m}

    bar = pltpu.get_barrier_semaphore()

    def greet_trow(j, _):
        pl.semaphore_signal(bar, inc=1, device_id={"trow": (r + 1 + j) % NR, "mode": m}, device_id_type=MESH)
        return 0

    def greet_mode(j, _):
        pl.semaphore_signal(bar, inc=1, device_id={"trow": r, "mode": (m + 1 + j) % NMODE}, device_id_type=MESH)
        return 0

    lax.fori_loop(0, NR - 1, greet_trow, 0)
    lax.fori_loop(0, NMODE - 1, greet_mode, 0)

    def fill():
        for load in loads[:2]:
            load.wait()

        def one(q, _):
            for i in range(2):
                t = rt[2 * q + i]
                for p in range(2):
                    for o in range(2):
                        sb[q, p, i, o] = g[p, o, t]
            return 0

        lax.fori_loop(0, NR, one, 0)
        rb[r] = sb[r]

    pl.semaphore_wait(bar, NR - 1 + NMODE - 1)

    swaps = [
        pltpu.make_async_remote_copy(
            c_hbm.at[:, i % 2, 4 * (1 - core) + i // 2], rhs.at[z, core, :, x, i], sw_s.at[i], sw_r.at[i],
            device_id={"trow": r, "mode": y * NCORE + 1 - core}, device_id_type=MESH,
        )
        for i in range(8)
    ]
    for swap in swaps:
        swap.start()

    def swapped():
        for copy in own_cols + swaps:
            copy.wait()

    sent = []

    def block(zz, xx, cols, half):
        h = slice(None) if half is None else half
        return rhs.at[zz, :, h, slice(None) if xx is None else xx, pl.ds(*cols)]

    def push(zz, xx, cols, half, ssem, rsem, dev):
        ref = block(zz, xx, cols, half)
        d = pltpu.make_async_remote_copy(ref, ref, ssem, rsem, device_id=dev, device_id_type=MESH)
        d.start()
        sent.append(d)

    def landed(zz, xx, cols, half, rsem):
        ref = block(zz, xx, cols, half)
        pltpu.make_async_copy(ref, ref, rsem).wait()

    up, down = trow_dev(at_z(1), x), trow_dev(at_z(-1), x)
    right, left = trow_dev(z, at_x(1)), trow_dev(z, at_x(-1))

    def z_send(t, xx, cols, ssem, rsem):
        lo, hi = (None, None) if t < 4 else (0, 1)
        push(at_z(-(t - 1)), xx, cols, lo, ssem.at[0, t - 1], rsem.at[0, t - 1], up)
        push(at_z(t - 1), xx, cols, hi, ssem.at[1, t - 1], rsem.at[1, t - 1], down)

    def z_wait(t, xx, cols, rsem):
        lo, hi = (None, None) if t < 4 else (0, 1)
        landed(at_z(-t), xx, cols, lo, rsem.at[0, t - 1])
        landed(at_z(t), xx, cols, hi, rsem.at[1, t - 1])

    def x_send(d, cols, ssem, rsem):
        push(at_z(d), x, cols, None, ssem.at[0], rsem.at[0], right)
        push(at_z(d), x, cols, None, ssem.at[1], rsem.at[1], left)

    def x_forward(d, cols, ssem, rsem):
        zz = at_z(d)
        landed(zz, at_x(-1), cols, None, rsem.at[0])
        push(zz, at_x(-1), cols, 0, ssem.at[2], rsem.at[2], right)
        landed(zz, at_x(1), cols, None, rsem.at[1])
        push(zz, at_x(1), cols, 1, ssem.at[3], rsem.at[3], left)

    def x_last(d, cols, rsem):
        zz = at_z(d)
        landed(zz, at_x(2), cols, 0, rsem.at[2])
        landed(zz, at_x(2), cols, 1, rsem.at[3])

    def za(ch):
        return za_s.at[ch], za_r.at[ch]

    def xa(ch, d):
        return xa_s.at[ch, d % NZ], xa_r.at[ch, d % NZ]

    def hop(ch, t):
        if t > 0:
            z_wait(t, x, A[ch], za(ch)[1])
        if t < 4:
            z_send(t + 1, x, A[ch], *za(ch))
        for d in {0: (0,), 4: (4,)}.get(t, (-t, t)):
            x_send(d, A[ch], *xa(ch, d))

    def forward(ch, t):
        for d in {0: (0,), 4: (4,)}.get(t, (-t, t)):
            x_forward(d, A[ch], *xa(ch, d))

    def last(ch, far):
        for d in FAR[far]:
            x_last(d, A[ch], xa(ch, d)[1])

    def x_first(ch, t):
        xb = (xb_s.at[ch], xb_r.at[ch])
        zb = (zb_s.at[ch], zb_r.at[ch])
        if t == 0:
            x_send(0, B[ch], *xb)
        if t == 1:
            x_forward(0, B[ch], *xb)
        if t == 2:
            x_last(0, B[ch], xb[1])
        if t >= 3:
            z_wait(t - 2, None, B[ch], zb[1])
        if 2 <= t <= 5:
            z_send(t - 1, None, B[ch], *zb)

    def mirror_send(d, e):
        q = at_z(d) * NX + at_x(e)
        pltpu.make_async_remote_copy(
            sb.at[q], rb.at[r], s1_send.at[0], s1_recv.at[r],
            device_id={"trow": q, "mode": m}, device_id_type=MESH,
        ).start()

    lane_group = lax.broadcasted_iota(jnp.int32, (16, 128), 1) // 16

    def mirror_regroup(d):
        kg = at_z(-d)
        for e in range(NX):
            if d == 0 and e == 0:
                continue
            q = kg * NX + at_x(-e)
            pltpu.make_async_copy(rb.at[q], rb.at[q], s1_recv.at[q]).wait()

        def one(ps, _):
            p, s = ps // 2, ps % 2
            tiles = [rb[kg * NX + k // 2, p, s, k % 2] for k in range(8)]
            for bit in (1, 2, 4):
                has = (lane_group // bit) % 2 == 1
                new = list(tiles)
                for k in range(8):
                    if k & bit:
                        continue
                    a, b = tiles[k], tiles[k + bit]
                    new[k] = jnp.where(has, pltpu.roll(b, 16 * bit, 1), a)
                    new[k + bit] = jnp.where(has, b, pltpu.roll(a, 128 - 16 * bit, 1))
                tiles = new
            for j in range(8):
                tb[kg, j, p, s] = tiles[j]
            return 0

        for ps in range(4):
            one(ps, 0)

        def send(j, _):
            to = (m + 1 + j) % NMODE
            pltpu.make_async_remote_copy(
                tb.at[kg, to], mb.at[kg, m], s2_send.at[0], s2_recv.at[kg, m],
                device_id={"trow": r, "mode": to}, device_id_type=MESH,
            ).start()
            return 0

        lax.fori_loop(0, NMODE - 1, send, 0)
        mb[kg, m] = tb[kg, m]

    def sigma(d):
        kg = at_z(-d)

        def arrive(j, _):
            q = (m + 1 + j) % NMODE
            pltpu.make_async_copy(mb.at[kg, q], mb.at[kg, q], s2_recv.at[kg, q]).wait()
            return 0

        lax.fori_loop(0, NMODE - 1, arrive, 0)
        base = pl.multiple_of(kg * 512 + core * 256, 256)
        for s in range(2):
            hr = mb[kg, :, 0, s].reshape(128, 128).astype(F32)
            hi = mb[kg, :, 1, s].reshape(128, 128).astype(F32)
            qr, qi = sq[kg, s, 0], sq[kg, s, 1]
            sr = qr * hr - qi * hi
            si = qr * hi + qi * hr
            lo, hi_lanes = pl.ds(base, 128), pl.ds(base + 128, 128)
            lhs[pl.ds(128 * s, 128), lo] = sr.astype(BF)
            lhs[pl.ds(128 * s, 128), hi_lanes] = (-si).astype(BF)
            lhs[pl.ds(256 + 128 * s, 128), lo] = si.astype(BF)
            lhs[pl.ds(256 + 128 * s, 128), hi_lanes] = sr.astype(BF)

        sigma_copy(d).start()

    def sigma_copy(d):
        here = lhs.at[:, pl.ds(pl.multiple_of(at_z(-d) * 512 + core * 256, 256), 256)]
        return pltpu.make_async_remote_copy(
            here, here, sg_s.at[d], sg_r.at[d],
            device_id={"trow": r, "mode": y * NCORE + 1 - core}, device_id_type=MESH,
        )

    def sigmas_landed(far):
        for d in FAR[far]:
            other = lhs.at[:, pl.ds(pl.multiple_of(at_z(-d) * 512 + (1 - core) * 256, 256), 256)]
            pltpu.make_async_copy(other, other, sg_r.at[d]).wait()

    def squares():
        loads[2].wait()
        loads[3].wait()

        def strengths(k, _):
            t = rt[k]
            row = dl[pl.ds(ds[t], 1), :]
            for s in range(2):
                live = jnp.where(t <= rt[2 * r + s], 1.0, 0.0).astype(F32)
                kb[s, k % 8, pl.ds(k // 8, 1), :] = row * live
            return 0

        lax.fori_loop(0, 64, strengths, 0)
        group8 = lax.broadcasted_iota(jnp.int32, (8, 128), 1) // 16
        for s in range(2):
            rows = jnp.zeros((8, 128), F32)
            for k in range(8):
                turned = pltpu.roll(kb[s, k], (16 * k + 128 - 16 * m) % 128, 1)
                rows = jnp.where(group8 == k, turned, rows)
            kb[s, 8] = rows
        cols = []
        for s in range(2):
            row = dl[pl.ds(ds[rt[2 * r + s]], 1), :]
            cols.append(jnp.broadcast_to(row, (128, 128)).T)

        def one(kg, _):
            for s in range(2):
                coupling = cols[s] * kb[s, 8, pl.ds(kg, 1), :]
                gr = sb[pl.ds(kg * NX, NX), 0, :, s].reshape(128, 128).astype(F32).T
                gi = sb[pl.ds(kg * NX, NX), 1, :, s].reshape(128, 128).astype(F32).T
                sq[kg, s, 0] = (gr * gr - gi * gi) * coupling
                sq[kg, s, 1] = (2.0 * gr * gi) * coupling
            return 0

        lax.fori_loop(0, NZ, one, 0)

    def sum_copy(j, e, other):
        here = pl.ds(FIRST[j], PIECE[j])
        ty, tc = (y + e) % NY, (1 - core if other else core)
        return pltpu.make_async_remote_copy(
            part16.at[:, here, ty, tc], gathered.at[other, e, :, here], sum_s.at[j, other, e], sum_r.at[j, other, e],
            device_id={"trow": r, "mode": ty * NCORE + tc}, device_id_type=MESH,
        )

    def multiply(j):
        def product(n, width):
            cols = jnp.concatenate([rhs[:, :, :, :, 2 * (n + w) : 2 * (n + w) + 2].reshape(4096, 128) for w in range(width)], axis=1)
            for h in range(2):
                rows = lhs[256 * h : 256 * (h + 1), :]
                acc = jnp.dot(rows, cols, preferred_element_type=F32)
                for s in range(2):
                    for w in range(width):
                        tile = acc[128 * s : 128 * (s + 1), 128 * w : 128 * (w + 1)].reshape(NY, NCORE, 16, 128)
                        part[2 * h + s, n + w] = tile
                        part16[2 * h + s, n + w] = tile.astype(BF)

        for i in range(PIECE[j] // 2):
            product(FIRST[j] + 2 * i, 2)
        if PIECE[j] % 2:
            product(FIRST[j] + PIECE[j] - 1, 1)
        for e, other in SUM_ORDER:
            sum_copy(j, e, other).start()

    def y_sum(j):
        for e, other in SUM_ORDER:
            sum_copy(j, e, other).wait_recv()
        here = pl.ds(FIRST[j], PIECE[j])
        mine = part[:, here, y, core]
        theirs = gathered[1, 0, :, here].astype(F32)
        for e in range(1, NY):
            mine += gathered[0, e, :, here].astype(F32)
            theirs += gathered[1, e, :, here].astype(F32)
        out[:, :, pl.ds(4 * core + FIRST[j], PIECE[j])] = (mine * SCALE).reshape(2, 2, PIECE[j], 16, 128)
        out[:, :, pl.ds(4 * (1 - core) + FIRST[j], PIECE[j])] = (theirs * SCALE).reshape(2, 2, PIECE[j], 16, 128)

    def sums_left(j):
        for e, other in SUM_ORDER:
            sum_copy(j, e, other).wait_send()

    def drain():
        for d in sent:
            d.wait_send()
        all_but_one = sb.at[pl.ds(0, NR - 1)]
        pltpu.make_async_copy(all_but_one, all_but_one, s1_send.at[0]).wait()
        all_but_own = tb.at[:, pl.ds(0, NMODE - 1)]
        pltpu.make_async_copy(all_but_own, all_but_own, s2_send.at[0]).wait()
        for d in range(NZ):
            sigma_copy(d).wait_send()
        for j in range(len(PIECE)):
            if j != LAST:
                sums_left(j)

    fill()
    mirror_send(5, 0)
    mirror_send(7, 2)
    mirror_send(2, 0)
    mirror_send(2, 3)
    mirror_send(0, 1)
    mirror_send(6, 3)
    mirror_send(1, 0)
    swapped()
    mirror_send(7, 3)
    hop(0, 0)
    mirror_send(5, 1)
    mirror_send(2, 2)
    mirror_send(3, 1)
    mirror_send(1, 1)
    mirror_send(3, 0)
    mirror_send(0, 2)
    mirror_send(6, 1)
    mirror_send(0, 3)
    x_first(1, 0)
    hop(1, 0)
    mirror_send(5, 2)
    hop(0, 1)
    mirror_send(7, 1)
    mirror_send(3, 2)
    mirror_send(1, 2)
    mirror_send(3, 3)
    x_first(1, 1)
    mirror_regroup(0)
    forward(0, 0)
    mirror_send(6, 0)
    mirror_send(1, 3)
    squares()
    mirror_send(5, 3)
    mirror_send(4, 1)
    mirror_send(6, 2)
    forward(0, 1)
    mirror_send(7, 0)
    hop(0, 2)
    hop(1, 1)
    mirror_send(2, 1)
    mirror_send(4, 2)
    mirror_regroup(5)
    mirror_send(4, 3)
    forward(1, 0)
    mirror_regroup(3)
    x_first(1, 2)
    forward(0, 2)
    mirror_regroup(6)
    mirror_regroup(1)
    sigma(5)
    hop(0, 3)
    mirror_send(4, 0)
    hop(1, 2)
    mirror_regroup(7)
    sigma(6)
    mirror_regroup(2)
    forward(0, 3)
    x_first(1, 3)
    sigma(1)
    hop(0, 4)
    mirror_regroup(4)
    hop(1, 3)
    sigma(0)
    x_first(1, 4)
    forward(0, 4)
    sigma(3)
    sigma(2)
    hop(1, 4)
    forward(1, 1)
    sigma(4)
    sigma(7)
    forward(1, 3)
    x_first(1, 5)
    last(0, 1)
    forward(1, 2)
    last(0, 0)
    forward(1, 4)
    sigmas_landed(1)
    sigmas_landed(0)
    multiply(0)
    last(1, 0)
    x_first(1, 6)
    last(1, 1)
    multiply(1)
    y_sum(0)
    drain()
    y_sum(1)

    sums_left(LAST)


def body(g_hist, new_cols, row_time, drive_step, drive_levels):
    hbm = pl.BlockSpec(memory_space=pltpu.HBM)
    operands = [
        pltpu.with_memory_space_constraint(v, pltpu.HBM)
        for v in (row_time, drive_step, drive_levels, g_hist, new_cols)
    ]
    vmem = pl.BlockSpec(memory_space=pltpu.VMEM)
    dma = pltpu.SemaphoreType.DMA
    return pl.pallas_call(
        kernel,
        out_shape=jax.ShapeDtypeStruct((2, 2, 8, 16, 128), F32),
        in_specs=[hbm] * 5,
        out_specs=vmem,
        scratch_shapes=[
            pltpu.SMEM((64,), jnp.int32),
            pltpu.SMEM((64,), jnp.int32),
            pltpu.VMEM((16, 128), F32),
            pltpu.VMEM((2, 2, 64, 16, 128), BF),
            pltpu.VMEM((NR, 2, 2, 2, 16, 128), BF),
            pltpu.VMEM((NR, 2, 2, 2, 16, 128), BF),
            pltpu.VMEM((NZ, NMODE, 2, 2, 16, 128), BF),
            pltpu.VMEM((NZ, NMODE, 2, 2, 16, 128), BF),
            pltpu.VMEM((NZ, 2, 2, 128, 128), F32),
            pltpu.VMEM((512, 4096), BF),
            pltpu.VMEM((NZ, NCORE, 2, NX, 8, 16, 128), BF),
            pltpu.VMEM((4, 4, NY, NCORE, 16, 128), F32),
            pltpu.VMEM((4, 4, NY, NCORE, 16, 128), BF),
            pltpu.VMEM((2, NY, 4, 4, 16, 128), BF),
            pltpu.VMEM((2, 9, 8, 128), F32),
            dma((4,)), dma((8,)), dma((1,)), dma((NR,)), dma((1,)), dma((NZ, NMODE)),
            dma((len(CHUNK), 2, 4)), dma((len(CHUNK), 2, 4)), dma((len(CHUNK), NZ, 4)), dma((len(CHUNK), NZ, 4)),
            dma((len(CHUNK), 4)), dma((len(CHUNK), 4)), dma((len(CHUNK), 2, 4)), dma((len(CHUNK), 2, 4)),
            dma((8,)), dma((8,)), dma((NZ,)), dma((NZ,)), dma((len(PIECE), 2, NY)), dma((len(PIECE), 2, NY)),
        ],
        compiler_params=pltpu.CompilerParams(
            collective_id=0, has_side_effects=True, vmem_limit_bytes=40 * 1024 * 1024
        ),
        cost_estimate=pl.CostEstimate(flops=2147483648, bytes_accessed=1600000, transcendentals=0),
    )(*operands)


def solution(mesh):
    placed = (
        P(None, "trow", None, "mode", None),
        P(None, "trow", None, "mode", None),
        P(),
        P(),
        P(),
    )
    return jax.shard_map(
        body,
        mesh=mesh,
        in_specs=placed,
        out_specs=P(None, "trow", None, "mode", None),
        check_vma=False,
    )
```

```python
import jax
import jax.numpy as jnp
from jax import lax
from jax.experimental import pallas as pl
from jax.experimental.pallas import tpu as pltpu
from jax.sharding import PartitionSpec as P

NZ, NX, NY, NCORE = 8, 4, 4, 2
NR, NMODE = NZ * NX, NY * NCORE
BF, F32 = jnp.bfloat16, jnp.float32
MESH = pl.DeviceIdType.MESH

CHUNK = ((4, 0), (3, 1))
PIECE = (2, 2)

SCALE = 8.0 / 64


def blocks(chunk, which):
    first = sum(a + b for a, b in CHUNK[:chunk]) + (CHUNK[chunk][0] if which else 0)
    return first, CHUNK[chunk][which]


A = [blocks(i, 0) for i in range(len(CHUNK))]
B = [blocks(i, 1) for i in range(len(CHUNK))]
LAST = 1
FAR = ((0, 1, 2, 6, 7), (3, 4, 5))
SUM_ORDER = ((2, 0), (2, 1), (1, 0), (3, 0), (1, 1), (3, 1), (0, 1))
FIRST = [sum(PIECE[:i]) for i in range(len(PIECE))]


def kernel(
    rt_hbm, ds_hbm, dl_hbm, g_hbm, c_hbm, out,
    rt, ds, dl, g, give,
    sb, rb, tb, mb, sq, lhs, rhs, part, part16, gathered, kb,
    in_sem, col_sem, s1_send, s1_recv, s2_send, s2_recv,
    za_s, za_r, xa_s, xa_r, xb_s, xb_r, zb_s, zb_r,
    own_s, sw_s, sw_r, sg_s, sg_r, sum_s, sum_r,
):
    r = lax.axis_index("trow")
    m = lax.axis_index("mode")
    z, x = r // NX, r % NX
    y, core = m // NCORE, m % NCORE
    loads = [
        pltpu.make_async_copy(src, dst, in_sem.at[i])
        for i, (src, dst) in enumerate(
            ((g_hbm, g), (rt_hbm, rt), (ds_hbm, ds), (dl_hbm, dl))
        )
    ]
    own_cols = [
        pltpu.make_async_copy(
            c_hbm.at[:, i % 2, 4 * core + i // 2], rhs.at[z, core, :, x, i], col_sem.at[i]
        )
        for i in range(8)
    ]
    give_cols = [
        pltpu.make_async_copy(
            c_hbm.at[:, i % 2, 4 * (1 - core) + i // 2], give.at[:, i], col_sem.at[8 + i]
        )
        for i in range(8)
    ]
    for load in own_cols + give_cols + loads:
        load.start()

    def at_z(d):
        return (z + d + NZ) % NZ

    def at_x(d):
        return (x + d + NX) % NX

    def row_of(zz, xx):
        return zz * NX + xx

    up_row, down_row = row_of(at_z(1), x), row_of(at_z(-1), x)
    right_row, left_row = row_of(z, at_x(1)), row_of(z, at_x(-1))

    bar = pltpu.get_barrier_semaphore()

    def greet_trow(j, _):
        pl.semaphore_signal(bar, inc=1, device_id={"trow": (r + 1 + j) % NR, "mode": m}, device_id_type=MESH)
        return 0

    def greet_mode(j, _):
        pl.semaphore_signal(bar, inc=1, device_id={"trow": r, "mode": (m + 1 + j) % NMODE}, device_id_type=MESH)
        return 0

    lax.fori_loop(0, NR - 1, greet_trow, 0)
    lax.fori_loop(0, NMODE - 1, greet_mode, 0)
    crossing = [{"trow": q, "mode": y * NCORE + 1 - core} for q in (up_row, down_row, right_row, left_row)]
    for dev in crossing:
        pl.semaphore_signal(bar, inc=1, device_id=dev, device_id_type=MESH)
    for copy in own_cols + give_cols:
        copy.wait()

    def fill():
        for load in loads[:2]:
            load.wait()

        def one(q, _):
            for i in range(2):
                t = rt[2 * q + i]
                for p in range(2):
                    for o in range(2):
                        sb[q, p, i, o] = g[p, o, t]
            return 0

        lax.fori_loop(0, NR, one, 0)
        rb[r] = sb[r]

    pl.semaphore_wait(bar, NR - 1 + NMODE - 1 + 4)

    swap = pltpu.make_async_remote_copy(
        give, rhs.at[z, core, :, x], sw_s.at[0], sw_r.at[0],
        device_id={"trow": r, "mode": y * NCORE + 1 - core}, device_id_type=MESH,
    )
    swap.start()

    def swapped():
        swap.wait()

    sent = []

    def block(zz, xx, cols, half):
        h = slice(None) if half is None else half
        return rhs.at[zz, :, h, slice(None) if xx is None else xx, pl.ds(*cols)]

    def push(zz, xx, cols, half, ssem, rsem, dev):
        ref = block(zz, xx, cols, half)
        d = pltpu.make_async_remote_copy(ref, ref, ssem, rsem, device_id=dev, device_id_type=MESH)
        d.start()
        sent.append(d)

    def landed(zz, xx, cols, half, rsem):
        ref = block(zz, xx, cols, half)
        pltpu.make_async_copy(ref, ref, rsem).wait()

    def push_own(cols, way, ssem, osem, rsem):
        row = (up_row, down_row, right_row, left_row)[way]
        dst = rhs.at[z, core, :, x, pl.ds(*cols)]
        for src, sem, dev in ((dst, ssem, {"trow": row, "mode": m}), (give.at[:, pl.ds(*cols)], osem, crossing[way])):
            d = pltpu.make_async_remote_copy(src, dst, sem, rsem, device_id=dev, device_id_type=MESH)
            d.start()
            sent.append(d)

    up, down = {"trow": up_row, "mode": m}, {"trow": down_row, "mode": m}
    right, left = {"trow": right_row, "mode": m}, {"trow": left_row, "mode": m}

    def z_send(t, xx, cols, ssem, rsem, osem=None):
        if osem is not None and t == 1:
            push_own(cols, 0, ssem.at[0, 0], osem.at[0], rsem.at[0, 0])
            push_own(cols, 1, ssem.at[1, 0], osem.at[1], rsem.at[1, 0])
            return
        lo, hi = (None, None) if t < 4 else (0, 1)
        push(at_z(-(t - 1)), xx, cols, lo, ssem.at[0, t - 1], rsem.at[0, t - 1], up)
        push(at_z(t - 1), xx, cols, hi, ssem.at[1, t - 1], rsem.at[1, t - 1], down)

    def z_wait(t, xx, cols, rsem):
        lo, hi = (None, None) if t < 4 else (0, 1)
        landed(at_z(-t), xx, cols, lo, rsem.at[0, t - 1])
        landed(at_z(t), xx, cols, hi, rsem.at[1, t - 1])

    def x_send(d, cols, ssem, rsem, osem):
        if d == 0:
            push_own(cols, 2, ssem.at[0], osem.at[0], rsem.at[0])
            push_own(cols, 3, ssem.at[1], osem.at[1], rsem.at[1])
            return
        push(at_z(d), x, cols, None, ssem.at[0], rsem.at[0], right)
        push(at_z(d), x, cols, None, ssem.at[1], rsem.at[1], left)

    def x_forward(d, cols, ssem, rsem):
        zz = at_z(d)
        landed(zz, at_x(-1), cols, None, rsem.at[0])
        push(zz, at_x(-1), cols, 0, ssem.at[2], rsem.at[2], right)
        landed(zz, at_x(1), cols, None, rsem.at[1])
        push(zz, at_x(1), cols, 1, ssem.at[3], rsem.at[3], left)

    def x_last(d, cols, rsem):
        zz = at_z(d)
        landed(zz, at_x(2), cols, 0, rsem.at[2])
        landed(zz, at_x(2), cols, 1, rsem.at[3])

    def za(ch):
        return za_s.at[ch], za_r.at[ch]

    def xa(ch, d):
        return xa_s.at[ch, d % NZ], xa_r.at[ch, d % NZ]

    def hop(ch, t):
        if t > 0:
            z_wait(t, x, A[ch], za(ch)[1])
        if t < 4:
            z_send(t + 1, x, A[ch], *za(ch), own_s.at[ch, 0])
        for d in {0: (0,), 4: (4,)}.get(t, (-t, t)):
            x_send(d, A[ch], *xa(ch, d), own_s.at[ch, 1])

    def forward(ch, t):
        for d in {0: (0,), 4: (4,)}.get(t, (-t, t)):
            x_forward(d, A[ch], *xa(ch, d))

    def last(ch, far):
        for d in FAR[far]:
            x_last(d, A[ch], xa(ch, d)[1])

    def x_first(ch, t):
        xb = (xb_s.at[ch], xb_r.at[ch])
        zb = (zb_s.at[ch], zb_r.at[ch])
        if t == 0:
            x_send(0, B[ch], *xb, own_s.at[ch, 2])
        if t == 1:
            x_forward(0, B[ch], *xb)
        if t == 2:
            x_last(0, B[ch], xb[1])
        if t >= 3:
            z_wait(t - 2, None, B[ch], zb[1])
        if 2 <= t <= 5:
            z_send(t - 1, None, B[ch], *zb)

    def mirror_send(d, e):
        q = at_z(d) * NX + at_x(e)
        pltpu.make_async_remote_copy(
            sb.at[q], rb.at[r], s1_send.at[0], s1_recv.at[r],
            device_id={"trow": q, "mode": m}, device_id_type=MESH,
        ).start()

    lane_group = lax.broadcasted_iota(jnp.int32, (16, 128), 1) // 16

    def mirror_regroup(d):
        kg = at_z(-d)
        for e in range(NX):
            if d == 0 and e == 0:
                continue
            q = kg * NX + at_x(-e)
            pltpu.make_async_copy(rb.at[q], rb.at[q], s1_recv.at[q]).wait()

        def one(ps, _):
            p, s = ps // 2, ps % 2
            tiles = [rb[kg * NX + k // 2, p, s, k % 2] for k in range(8)]
            for bit in (1, 2, 4):
                has = (lane_group // bit) % 2 == 1
                new = list(tiles)
                for k in range(8):
                    if k & bit:
                        continue
                    a, b = tiles[k], tiles[k + bit]
                    new[k] = jnp.where(has, pltpu.roll(b, 16 * bit, 1), a)
                    new[k + bit] = jnp.where(has, b, pltpu.roll(a, 128 - 16 * bit, 1))
                tiles = new
            for j in range(8):
                tb[kg, j, p, s] = tiles[j]
            return 0

        for ps in range(4):
            one(ps, 0)

        def send(j, _):
            to = (m + 1 + j) % NMODE
            pltpu.make_async_remote_copy(
                tb.at[kg, to], mb.at[kg, m], s2_send.at[0], s2_recv.at[kg, m],
                device_id={"trow": r, "mode": to}, device_id_type=MESH,
            ).start()
            return 0

        lax.fori_loop(0, NMODE - 1, send, 0)
        mb[kg, m] = tb[kg, m]

    def sigma(d):
        kg = at_z(-d)

        def arrive(j, _):
            q = (m + 1 + j) % NMODE
            pltpu.make_async_copy(mb.at[kg, q], mb.at[kg, q], s2_recv.at[kg, q]).wait()
            return 0

        lax.fori_loop(0, NMODE - 1, arrive, 0)
        base = pl.multiple_of(kg * 512 + core * 256, 256)
        for s in range(2):
            hr = mb[kg, :, 0, s].reshape(128, 128).astype(F32)
            hi = mb[kg, :, 1, s].reshape(128, 128).astype(F32)
            qr, qi = sq[kg, s, 0], sq[kg, s, 1]
            sr = qr * hr - qi * hi
            si = qr * hi + qi * hr
            lo, hi_lanes = pl.ds(base, 128), pl.ds(base + 128, 128)
            lhs[pl.ds(128 * s, 128), lo] = sr.astype(BF)
            lhs[pl.ds(128 * s, 128), hi_lanes] = (-si).astype(BF)
            lhs[pl.ds(256 + 128 * s, 128), lo] = si.astype(BF)
            lhs[pl.ds(256 + 128 * s, 128), hi_lanes] = sr.astype(BF)

        sigma_copy(d).start()

    def sigma_copy(d):
        here = lhs.at[:, pl.ds(pl.multiple_of(at_z(-d) * 512 + core * 256, 256), 256)]
        return pltpu.make_async_remote_copy(
            here, here, sg_s.at[d], sg_r.at[d],
            device_id={"trow": r, "mode": y * NCORE + 1 - core}, device_id_type=MESH,
        )

    def sigmas_landed(far):
        for d in FAR[far]:
            other = lhs.at[:, pl.ds(pl.multiple_of(at_z(-d) * 512 + (1 - core) * 256, 256), 256)]
            pltpu.make_async_copy(other, other, sg_r.at[d]).wait()

    def squares():
        loads[2].wait()
        loads[3].wait()

        def strengths(k, _):
            t = rt[k]
            row = dl[pl.ds(ds[t], 1), :]
            for s in range(2):
                live = jnp.where(t <= rt[2 * r + s], 1.0, 0.0).astype(F32)
                kb[s, k % 8, pl.ds(k // 8, 1), :] = row * live
            return 0

        lax.fori_loop(0, 64, strengths, 0)
        group8 = lax.broadcasted_iota(jnp.int32, (8, 128), 1) // 16
        for s in range(2):
            rows = jnp.zeros((8, 128), F32)
            for k in range(8):
                turned = pltpu.roll(kb[s, k], (16 * k + 128 - 16 * m) % 128, 1)
                rows = jnp.where(group8 == k, turned, rows)
            kb[s, 8] = rows
        cols = []
        for s in range(2):
            row = dl[pl.ds(ds[rt[2 * r + s]], 1), :]
            cols.append(jnp.broadcast_to(row, (128, 128)).T)

        def one(kg, _):
            for s in range(2):
                coupling = cols[s] * kb[s, 8, pl.ds(kg, 1), :]
                gr = sb[pl.ds(kg * NX, NX), 0, :, s].reshape(128, 128).astype(F32).T
                gi = sb[pl.ds(kg * NX, NX), 1, :, s].reshape(128, 128).astype(F32).T
                sq[kg, s, 0] = (gr * gr - gi * gi) * coupling
                sq[kg, s, 1] = (2.0 * gr * gi) * coupling
            return 0

        lax.fori_loop(0, NZ, one, 0)

    def sum_copy(j, e, other):
        here = pl.ds(FIRST[j], PIECE[j])
        ty, tc = (y + e) % NY, (1 - core if other else core)
        return pltpu.make_async_remote_copy(
            part16.at[:, here, ty, tc], gathered.at[other, e, :, here], sum_s.at[j, other, e], sum_r.at[j, other, e],
            device_id={"trow": r, "mode": ty * NCORE + tc}, device_id_type=MESH,
        )

    def multiply(j):
        def product(n, width):
            cols = jnp.concatenate([rhs[:, :, :, :, 2 * (n + w) : 2 * (n + w) + 2].reshape(4096, 128) for w in range(width)], axis=1)
            for h in range(2):
                rows = lhs[256 * h : 256 * (h + 1), :]
                acc = jnp.dot(rows, cols, preferred_element_type=F32)
                for s in range(2):
                    for w in range(width):
                        tile = acc[128 * s : 128 * (s + 1), 128 * w : 128 * (w + 1)].reshape(NY, NCORE, 16, 128)
                        part[2 * h + s, n + w] = tile
                        part16[2 * h + s, n + w] = tile.astype(BF)

        for i in range(PIECE[j] // 2):
            product(FIRST[j] + 2 * i, 2)
        if PIECE[j] % 2:
            product(FIRST[j] + PIECE[j] - 1, 1)
        for e, other in SUM_ORDER:
            sum_copy(j, e, other).start()

    def y_sum(j):
        for e, other in SUM_ORDER:
            sum_copy(j, e, other).wait_recv()
        here = pl.ds(FIRST[j], PIECE[j])
        mine = part[:, here, y, core]
        theirs = gathered[1, 0, :, here].astype(F32)
        for e in range(1, NY):
            mine += gathered[0, e, :, here].astype(F32)
            theirs += gathered[1, e, :, here].astype(F32)
        out[:, :, pl.ds(4 * core + FIRST[j], PIECE[j])] = (mine * SCALE).reshape(2, 2, PIECE[j], 16, 128)
        out[:, :, pl.ds(4 * (1 - core) + FIRST[j], PIECE[j])] = (theirs * SCALE).reshape(2, 2, PIECE[j], 16, 128)

    def sums_left(j):
        for e, other in SUM_ORDER:
            sum_copy(j, e, other).wait_send()

    def drain():
        for d in sent:
            d.wait_send()
        all_but_one = sb.at[pl.ds(0, NR - 1)]
        pltpu.make_async_copy(all_but_one, all_but_one, s1_send.at[0]).wait()
        all_but_own = tb.at[:, pl.ds(0, NMODE - 1)]
        pltpu.make_async_copy(all_but_own, all_but_own, s2_send.at[0]).wait()
        for d in range(NZ):
            sigma_copy(d).wait_send()
        for j in range(len(PIECE)):
            if j != LAST:
                sums_left(j)

    hop(0, 0)
    fill()
    mirror_send(0, 3)
    hop(1, 0)
    mirror_send(5, 0)
    mirror_send(3, 0)
    mirror_send(6, 0)
    mirror_send(4, 2)
    mirror_send(2, 2)
    swapped()
    mirror_send(5, 2)
    squares()
    mirror_send(1, 1)
    hop(0, 1)
    x_first(1, 0)
    mirror_send(7, 3)
    mirror_send(6, 3)
    mirror_send(2, 1)
    mirror_send(6, 2)
    mirror_send(2, 0)
    mirror_send(0, 1)
    mirror_send(2, 3)
    mirror_send(1, 3)
    mirror_send(6, 1)
    hop(1, 1)
    mirror_send(4, 1)
    mirror_send(7, 1)
    mirror_send(1, 0)
    mirror_send(0, 2)
    hop(0, 2)
    mirror_send(7, 2)
    mirror_regroup(2)
    mirror_send(1, 2)
    mirror_send(3, 2)
    mirror_send(3, 3)
    mirror_send(5, 1)
    x_first(1, 1)
    mirror_regroup(0)
    mirror_send(7, 0)
    mirror_send(5, 3)
    mirror_send(4, 3)
    forward(0, 0)
    mirror_send(3, 1)
    hop(0, 3)
    forward(0, 1)
    forward(1, 1)
    mirror_regroup(6)
    x_first(1, 2)
    forward(0, 2)
    mirror_regroup(1)
    mirror_regroup(7)
    forward(0, 3)
    mirror_regroup(5)
    mirror_send(4, 0)
    hop(1, 2)
    mirror_regroup(3)
    sigma(7)
    hop(0, 4)
    x_first(1, 3)
    sigma(0)
    sigma(2)
    forward(1, 0)
    mirror_regroup(4)
    hop(1, 3)
    sigma(6)
    sigma(5)
    x_first(1, 4)
    sigma(1)
    forward(0, 4)
    sigma(3)
    last(0, 0)
    hop(1, 4)
    sigma(4)
    forward(1, 2)
    sigmas_landed(0)
    forward(1, 3)
    last(0, 1)
    x_first(1, 5)
    forward(1, 4)
    sigmas_landed(1)
    multiply(0)
    last(1, 0)
    x_first(1, 6)
    last(1, 1)
    multiply(1)
    y_sum(0)
    drain()
    y_sum(1)

    sums_left(LAST)


def body(g_hist, new_cols, row_time, drive_step, drive_levels):
    hbm = pl.BlockSpec(memory_space=pltpu.HBM)
    operands = [
        pltpu.with_memory_space_constraint(v, pltpu.HBM)
        for v in (row_time, drive_step, drive_levels, g_hist, new_cols)
    ]
    vmem = pl.BlockSpec(memory_space=pltpu.VMEM)
    dma = pltpu.SemaphoreType.DMA
    return pl.pallas_call(
        kernel,
        out_shape=jax.ShapeDtypeStruct((2, 2, 8, 16, 128), F32),
        in_specs=[hbm] * 5,
        out_specs=vmem,
        scratch_shapes=[
            pltpu.SMEM((64,), jnp.int32),
            pltpu.SMEM((64,), jnp.int32),
            pltpu.VMEM((16, 128), F32),
            pltpu.VMEM((2, 2, 64, 16, 128), BF),
            pltpu.VMEM((2, 8, 16, 128), BF),
            pltpu.VMEM((NR, 2, 2, 2, 16, 128), BF),
            pltpu.VMEM((NR, 2, 2, 2, 16, 128), BF),
            pltpu.VMEM((NZ, NMODE, 2, 2, 16, 128), BF),
            pltpu.VMEM((NZ, NMODE, 2, 2, 16, 128), BF),
            pltpu.VMEM((NZ, 2, 2, 128, 128), F32),
            pltpu.VMEM((512, 4096), BF),
            pltpu.VMEM((NZ, NCORE, 2, NX, 8, 16, 128), BF),
            pltpu.VMEM((4, 4, NY, NCORE, 16, 128), F32),
            pltpu.VMEM((4, 4, NY, NCORE, 16, 128), BF),
            pltpu.VMEM((2, NY, 4, 4, 16, 128), BF),
            pltpu.VMEM((2, 9, 8, 128), F32),
            dma((4,)), dma((16,)), dma((1,)), dma((NR,)), dma((1,)), dma((NZ, NMODE)),
            dma((len(CHUNK), 2, 4)), dma((len(CHUNK), 2, 4)), dma((len(CHUNK), NZ, 4)), dma((len(CHUNK), NZ, 4)),
            dma((len(CHUNK), 4)), dma((len(CHUNK), 4)), dma((len(CHUNK), 2, 4)), dma((len(CHUNK), 2, 4)),
            dma((len(CHUNK), 3, 2)), dma((1,)), dma((1,)), dma((NZ,)), dma((NZ,)), dma((len(PIECE), 2, NY)), dma((len(PIECE), 2, NY)),
        ],
        compiler_params=pltpu.CompilerParams(
            collective_id=0, has_side_effects=True, vmem_limit_bytes=40 * 1024 * 1024
        ),
        cost_estimate=pl.CostEstimate(flops=2147483648, bytes_accessed=1600000, transcendentals=0),
    )(*operands)


def solution(mesh):
    placed = (
        P(None, "trow", None, "mode", None),
        P(None, "trow", None, "mode", None),
        P(),
        P(),
        P(),
    )
    return jax.shard_map(
        body,
        mesh=mesh,
        in_specs=placed,
        out_specs=P(None, "trow", None, "mode", None),
        check_vma=False,
    )
```
